128 devices in a mesh: space: 16 (over y, x_lo, core), chan: 4 (over z), filt: 2 (over x_hi).
Axes of the slice: x: 4 (x_hi: 2, x_lo: 2; x = x_hi * 2 + x_lo), y: 4, z: 4, core: 2. Of those that a mesh axis runs over, the one named last changes fastest.
Arguments:
- volume: bfloat16 [64, 32, 32, 512], P('space', None, None, 'chan'), may hold values from -6 to 6
- kernel_one: bfloat16 [27, 512, 1024], P(None, 'chan', 'filt'), may hold values from -0.0546875 to 0.0546875
- kernel_two: bfloat16 [27, 1024, 1024], P(None, 'filt', 'chan'), may hold values from -0.0390625 to 0.0390625
- upstream: bfloat16 [16, 8, 8, 1024], P('space', None, None, ('chan', 'filt')), may hold values from -0.23925781 to 0.23925781
Outputs:
- features: float32 [16, 8, 8, 1024], P('space', None, None, ('chan', 'filt'))
- kernel_one_grad: float32 [27, 512, 1024], P(None, ('chan', 'space'), 'filt')
- kernel_two_grad: float32 [27, 1024, 1024], P(None, ('filt', 'space'), 'chan')
The draws below stay inside these ranges and needn't reach their ends.
All inputs are finite; a program needn't handle non-finite values.
Results may differ from the reference program's by a relative error of at most 0.005.
Values may be sent and summed in bfloat16 or wider, within the bound.
A program may use at most 128 MiB of HBM per device.

```python
import jax
import jax.numpy as jnp
from jax import lax

CIN = 512
CMID = 1024
COUT = 1024
SIDE = 32
IN_PLANES = 64
OUT_PLANES = 16


def block_scale(rng, dims, cuts, smallest, top_value):
    gain, own = 1.0, jax.random.fold_in(rng, 6)
    for axis_at, parts in cuts:
        draws = jnp.exp(jax.random.uniform(jax.random.fold_in(own, axis_at), (parts,), jnp.float32, smallest / len(cuts), top_value / len(cuts)))
        gain = gain * jnp.repeat(draws, dims[axis_at] // parts).reshape([-1 if axis == axis_at else 1 for axis in range(len(dims))])
    return gain


def centred(rng, dims, scale, reach, split=(), held_as=jnp.bfloat16):
    entries = scale * jax.random.normal(rng, dims, jnp.float32)
    if split:
        entries = entries * block_scale(rng, dims, split, -0.22, 0.18)
    return jnp.clip(entries, -reach, reach).astype(held_as)


def setup_inputs(seed: int = 0) -> dict:
    keys = jax.random.split(jax.random.key(seed), 5)
    return {
        "volume": centred(keys[0], (IN_PLANES, SIDE, SIDE, CIN), 1.0, 6.0, ((0, 16), (3, 4))),
        "kernel_one": centred(keys[1], (27, CIN, CMID), (27 * CIN) ** -0.5, 0.0546875, ((1, 4), (2, 2))),
        "kernel_two": centred(keys[2], (27, CMID, COUT), (27 * CMID) ** -0.5, 0.0390625, ((1, 2), (2, 4))),
        "upstream": centred(keys[3], (OUT_PLANES, SIDE // 4, SIDE // 4, COUT), 0.04, 0.23925781, ((0, 16), (3, 8))),
    }


LEAKY_SLOPE = 0.3


def patches(padded, depth_out, side_out):
    channels = padded.shape[3]
    pieces = []
    for depth_tap in range(3):
        for row_tap in range(3):
            for col_tap in range(3):
                pieces.append(lax.slice(padded, (depth_tap, row_tap, col_tap, 0), (depth_tap + 2 * depth_out - 1, row_tap + 2 * side_out - 1, col_tap + 2 * side_out - 1, channels), (2, 2, 2, 1)))
    return jnp.stack(pieces, axis=3).reshape(depth_out * side_out * side_out, 27 * channels)


def spread(columns, depth_out, side_out):
    channels = columns.shape[1] // 27
    blocks = columns.reshape(depth_out, side_out, side_out, 27, channels)
    running = jnp.zeros((2 * depth_out + 1, 2 * side_out + 1, 2 * side_out + 1, channels), columns.dtype)
    zero_value = jnp.zeros((), columns.dtype)
    tap_index = 0
    for depth_tap in range(3):
        for row_tap in range(3):
            for col_tap in range(3):
                running = running + lax.pad(blocks[:, :, :, tap_index, :], zero_value, ((depth_tap, 2 - depth_tap, 1), (row_tap, 2 - row_tap, 1), (col_tap, 2 - col_tap, 1), (0, 0, 0)))
                tap_index += 1
    return running


def reference(volume, kernel_one, kernel_two, upstream):
    in_channels = volume.shape[3]
    mid_channels = kernel_one.shape[2]
    out_channels = kernel_two.shape[2]
    planes_mid = volume.shape[0] // 2
    side_mid = volume.shape[1] // 2
    padded = jnp.pad(volume, ((1, 0), (1, 0), (1, 0), (0, 0)))
    patch_one = patches(padded, planes_mid, side_mid)
    mixed_sum = jnp.dot(patch_one, kernel_one.reshape(27 * in_channels, mid_channels), preferred_element_type=jnp.float32)
    hidden = jnp.where(mixed_sum > 0, mixed_sum, LEAKY_SLOPE * mixed_sum).astype(jnp.bfloat16)
    hidden_vol = hidden.reshape(planes_mid, side_mid, side_mid, mid_channels)
    hidden_padded = jnp.pad(hidden_vol, ((1, 0), (1, 0), (1, 0), (0, 0)))
    planes_out = planes_mid // 2
    side_out = side_mid // 2
    patch_two = patches(hidden_padded, planes_out, side_out)
    kernel_flat = kernel_two.reshape(27 * mid_channels, out_channels)
    features = jnp.dot(patch_two, kernel_flat, preferred_element_type=jnp.float32).reshape(planes_out, side_out, side_out, out_channels)
    seed_rows = upstream.reshape(-1, out_channels)
    kernel_two_grad = lax.dot_general(patch_two, seed_rows, (((0,), (0,)), ((), ())), preferred_element_type=jnp.float32).reshape(27, mid_channels, out_channels)
    back_columns = lax.dot_general(seed_rows, kernel_flat, (((1,), (1,)), ((), ())), preferred_element_type=jnp.float32)
    back_full = spread(back_columns, planes_out, side_out)[1:, 1:, 1:]
    delta_full = (back_full.reshape(-1, mid_channels) * jnp.where(mixed_sum > 0, 1.0, LEAKY_SLOPE)).astype(jnp.bfloat16)
    kernel_one_grad = lax.dot_general(patch_one, delta_full, (((0,), (0,)), ((), ())), preferred_element_type=jnp.float32).reshape(27, in_channels, mid_channels)
    return features, kernel_one_grad, kernel_two_grad
```

```python
import jax
import jax.numpy as jnp
from jax import lax
from jax.experimental import pallas as pl
from jax.experimental.pallas import tpu as pltpu
from jax.sharding import PartitionSpec as P

SLOPE = 0.3
F32, BF16 = jnp.float32, jnp.bfloat16
MESH = pl.DeviceIdType.MESH
NMSG = 64


def tap_parts(tap):
    return tap // 9, (tap // 3) % 3, tap % 3


def tap_phase(tap):
    a, b, c = tap_parts(tap)
    return ((a != 1) * 2 + (b != 1)) * 2 + (c != 1)


def tap_shift(tap):
    return tuple(int(v == 0) for v in tap_parts(tap))


def body(
    vol, k1, k2, up, feat_o, g1_o, g2_o,
    vol_v, halo_v, k1_v, k2_v, pf, patch, patch_t,
    up_all, up_f, up_s,
    part, mr1, mr2, bpart, bs1, bs2, br1, br2,
    hid, dlt,
    acc, ksend, krecv, accx, xs4, xr4, xs1, xr1, ys1, yr1, ys2, yr2,
    gh, hh, hp, fs, fp, fr, fx, fxr,
    lsem, ssem, rsem,
):
    s, z, h = lax.axis_index("space"), lax.axis_index("chan"), lax.axis_index("filt")
    k, pair = lax.rem(s, 2), lax.div(s, 2)
    xl, y = lax.rem(pair, 2), lax.div(pair, 2)
    zp, zm, z2 = lax.rem(z + 1, 4), lax.rem(z + 3, 4), lax.rem(z + 2, 4)
    yp, ym, y2 = lax.rem(y + 1, 4), lax.rem(y + 3, 4), lax.rem(y + 2, 4)
    sib = {"space": s + 1 - 2 * k}
    xpt = {"space": y * 4 + (1 - xl) * 2 + k}
    hpt = {"filt": 1 - h}
    yup, ydn, yfar = ({"space": v * 4 + xl * 2 + k} for v in (yp, ym, y2))
    zup, zdn = {"chan": zp}, {"chan": zm}
    nxt, prv = {"space": lax.rem(s + 1, 16)}, {"space": lax.rem(s + 15, 16)}

    msgs = {}

    def send(name, src, dst, device):
        i = len(msgs)
        msgs[name] = pltpu.make_async_remote_copy(
            src_ref=src, dst_ref=dst, send_sem=ssem.at[i], recv_sem=rsem.at[i], device_id=device, device_id_type=MESH
        )
        msgs[name].start()

    def got(name):
        msgs[name].wait_recv()

    def lanes(q):
        return pl.ds(pl.multiple_of(q * 128, 128), 128)

    loads = [
        pltpu.make_async_copy(vol, vol_v, lsem.at[0]),
        pltpu.make_async_copy(up, up_all.at[h, s], lsem.at[1]),
        pltpu.make_async_copy(k1, k1_v, lsem.at[2]),
        pltpu.make_async_copy(k2, k2_v, lsem.at[3]),
    ]
    for copy in loads:
        copy.start()

    barrier = pltpu.get_barrier_semaphore()
    around = (sib, xpt, hpt, yup, ydn, yfar, zup, zdn, nxt, prv)
    for device in around:
        pl.semaphore_signal(barrier, inc=1, device_id=device, device_id_type=MESH)
    pl.semaphore_wait(barrier, len(around))

    send("halo", vol.at[3], halo_v, nxt)
    loads[1].wait()
    send("u1", up_all.at[h, s], up_all.at[h, s], sib)

    zero_row = jnp.zeros((40, 128), F32)
    zero_col = jnp.zeros((33, 8, 128), F32)
    for p in range(5):
        pf[p, 0] = zero_row
        pf[p, :, 0:8, :] = zero_col
    loads[0].wait()

    def widen(r, carry):
        for p in range(4):
            pf[p + 1, r + 1, 8:40, :] = vol_v[p, r].astype(F32)
        return carry

    lax.fori_loop(0, 32, widen, 0)

    def build(o, depth_taps):
        def step(n, carry):
            pi, ii = lax.div(n, 4), lax.rem(n, 4)
            for pj in range(2):
                base = pl.multiple_of((o * 4 + pi * 2 + pj) * 64 + ii * 16, 16)
                for a in depth_taps:
                    for b in range(3):
                        row = 8 * ii + 2 * pi + b
                        for c in range(3):
                            tap = 9 * a + 3 * b + c
                            cols = pl.ds(7 + 2 * pj + c, 8, stride=4)
                            both = [pf[2 * o + a, row + 4 * e, cols, :] for e in range(2)]
                            patch[pl.ds(base, 16), tap * 128 : (tap + 1) * 128] = jnp.concatenate(both, 0).astype(BF16)
            return carry

        lax.fori_loop(0, 8, step, 0)

    build(1, (0, 1, 2))
    got("u1")
    two = pl.ds(pair * 2, 2)
    send("u2", up_all.at[h, two], up_all.at[h, two], xpt)
    build(0, (1, 2))
    got("u2")
    four = pl.ds(y * 4, 4)
    send("u3", up_all.at[h, four], up_all.at[h, four], hpt)
    got("halo")

    def widen_halo(r, carry):
        pf[0, r + 1, 8:40, :] = jnp.where(s > 0, halo_v[r].astype(F32), 0.0)
        return carry

    lax.fori_loop(0, 32, widen_halo, 0)
    build(0, (0,))
    got("u3")
    send("u4p", up_all.at[:, four], up_all.at[:, four], yup)
    send("u4m", up_all.at[:, four], up_all.at[:, four], ydn)

    loads[2].wait()

    def conv_one(away):
        q = lax.rem(z + away, 4)

        def step(half, carry):
            rows = pl.ds(pl.multiple_of(half * 256, 256), 256)
            part[away, rows, :] = jnp.dot(patch[rows, :], k1_v[:, lanes(q)], preferred_element_type=F32)
            return carry

        lax.fori_loop(0, 2, step, 0)

    low, high = pl.ds(0, 256), pl.ds(256, 256)
    conv_one(2)
    send("m1p", part.at[2, low], mr1.at[0], zup)
    send("m1m", part.at[2, high], mr1.at[1], zdn)
    conv_one(1)
    send("m2pb", part.at[1, high], mr2.at[0, high], zup)
    conv_one(3)
    send("m2ma", part.at[3, low], mr2.at[1, low], zdn)
    got("m1p")
    part[1, 0:256] += mr1[0]
    send("m2pa", part.at[1, low], mr2.at[0, low], zup)
    got("m1m")
    part[3, 256:512] += mr1[1]
    send("m2mb", part.at[3, high], mr2.at[1, high], zdn)
    conv_one(0)

    got("u4p")
    got("u4m")
    below, above = pl.ds(ym * 4, 4), pl.ds(yp * 4, 4)
    send("u5p", up_all.at[0, below], up_all.at[0, below], yup)
    send("u5m", up_all.at[1, above], up_all.at[1, above], ydn)
    up_f[...] = jnp.zeros_like(up_f)
    for d in range(4):
        up_s[d, 1024:1088, :] = jnp.zeros((64, 256), BF16)
    got("u5p")
    got("u5m")

    def shifted(slab, carry):
        for half in range(2):
            up_f[0:8, 0:8, half * 128 : (half + 1) * 128] = up_all[half, slab].astype(F32).reshape(8, 8, 128)
        rows = pl.ds(pl.multiple_of(slab * 64, 64), 64)
        for di in range(2):
            for dj in range(2):
                up_s[di * 2 + dj, rows, :] = up_f[di : di + 8, dj : dj + 8, :].reshape(64, 256).astype(BF16)
        return carry

    lax.fori_loop(0, 16, shifted, 0)

    loads[3].wait()
    for phase in range(8):
        total = None
        for tap in range(27):
            if tap_phase(tap) != phase:
                continue
            do, di, dj = tap_shift(tap)
            rows = pl.ds(pl.multiple_of((s + do) * 64, 64), 64)
            term = lax.dot_general(
                up_s[di * 2 + dj, rows, :],
                k2_v[tap * 512 : (tap + 1) * 512, :],
                (((1,), (1,)), ((), ())),
                preferred_element_type=F32,
            )
            total = term if total is None else total + term
        for q in range(4):
            bpart[q, phase * 64 : (phase + 1) * 64, :] = total[:, q * 128 : (q + 1) * 128]
    bs1[...] = bpart[z2].astype(BF16)
    send("b1p", bs1.at[low], br1.at[0], zup)
    send("b1m", bs1.at[high], br1.at[1], zdn)
    bs2[0, 256:512] = bpart[zp, 256:512].astype(BF16)
    send("b2pb", bs2.at[0, high], br2.at[0, high], zup)
    bs2[1, 0:256] = bpart[zm, 0:256].astype(BF16)
    send("b2ma", bs2.at[1, low], br2.at[1, low], zdn)

    def turn(n, carry):
        flat = patch[:, pl.ds(pl.multiple_of(n * 256, 256), 256)].astype(F32).T
        rows = pl.ds(pl.multiple_of(n * 16, 16), 16)
        for owner in range(16):
            both = [flat[e * 128 + owner * 8 : e * 128 + owner * 8 + 8] for e in range(2)]
            patch_t[owner, rows, :] = jnp.concatenate(both, 0).astype(BF16)
        return carry

    lax.fori_loop(0, 13, turn, 0)
    flat = patch[:, 26 * 128 : 27 * 128].astype(F32).T
    for owner in range(16):
        both = [flat[owner * 8 : owner * 8 + 8], jnp.zeros((8, 512), F32)]
        patch_t[owner, 208:224, :] = jnp.concatenate(both, 0).astype(BF16)

    got("b1p")
    bs2[0, 0:256] = (bpart[zp, 0:256] + br1[0].astype(F32)).astype(BF16)
    send("b2pa", bs2.at[0, low], br2.at[0, low], zup)
    got("b1m")
    bs2[1, 256:512] = (bpart[zm, 256:512] + br1[1].astype(F32)).astype(BF16)
    send("b2mb", bs2.at[1, high], br2.at[1, high], zdn)

    for name in ("m2pb", "m2ma", "m2pa", "m2mb"):
        got(name)
    mixed = part[0] + mr2[0] + mr2[1]
    part[0] = mixed
    hid[:, lanes(z)] = jnp.where(mixed > 0, mixed, SLOPE * mixed).astype(BF16)
    send("h1p", hid.at[:, lanes(z)], hid.at[:, lanes(z)], zup)
    send("h1m", hid.at[:, lanes(z)], hid.at[:, lanes(z)], zdn)
    for name in ("b2pb", "b2ma", "b2pa", "b2mb"):
        got(name)
    back = bpart[z] + br2[0].astype(F32) + br2[1].astype(F32)
    dlt[:, lanes(z)] = (back * jnp.where(part[0] > 0, 1.0, SLOPE)).astype(BF16)
    send("d1p", dlt.at[:, lanes(z)], dlt.at[:, lanes(z)], zup)
    send("d1m", dlt.at[:, lanes(z)], dlt.at[:, lanes(z)], zdn)

    def grad_one(slot):
        q = lax.rem(z + slot, 4)

        def away(n, carry):
            rows = pl.ds(pl.multiple_of(lax.rem(n, 2) * 224, 32), 224)
            term = jnp.dot(patch_t[2 * n + 1 - k], dlt[:, lanes(q)], preferred_element_type=F32)
            ksend[slot, lax.div(n, 2), rows, :] = term.astype(BF16)
            return carry

        def kept(n, carry):
            rows = pl.ds(pl.multiple_of(lax.rem(n, 2) * 224, 32), 224)
            term = jnp.dot(patch_t[2 * n + k], dlt[:, lanes(q)], preferred_element_type=F32)
            acc[slot, lax.div(n, 2), rows, :] = term
            return carry

        lax.fori_loop(0, 8, away, 0)
        send(f"k{slot}", ksend.at[slot], krecv.at[slot], sib)
        lax.fori_loop(0, 8, kept, 0)

    def add_sibling(slot):
        got(f"k{slot}")

        def step(n, carry):
            acc[slot, n] += krecv[slot, n].astype(F32)
            return carry

        lax.fori_loop(0, 4, step, 0)

    def y_first(slot, ref, rows):
        half = rows // 2
        ys1[slot, 0:rows] = ref[y2].astype(BF16)
        send(f"p{slot}", ys1.at[slot, 0:half], yr1.at[slot, 0, 0:half], yup)
        send(f"q{slot}", ys1.at[slot, half:rows], yr1.at[slot, 1, 0:half], ydn)

    def y_second(slot, ref, rows):
        half = rows // 2
        got(f"p{slot}")
        ys2[slot, 0, 0:half] = (ref[yp, 0:half] + yr1[slot, 0, 0:half].astype(F32)).astype(BF16)
        ys2[slot, 0, half:rows] = ref[yp, half:rows].astype(BF16)
        send(f"r{slot}", ys2.at[slot, 0, 0:rows], yr2.at[slot, 0, 0:rows], yup)
        got(f"q{slot}")
        ys2[slot, 1, 0:half] = ref[ym, 0:half].astype(BF16)
        ys2[slot, 1, half:rows] = (ref[ym, half:rows] + yr1[slot, 1, 0:half].astype(F32)).astype(BF16)
        send(f"t{slot}", ys2.at[slot, 1, 0:rows], yr2.at[slot, 1, 0:rows], ydn)

    def y_third(slot, ref, rows):
        got(f"r{slot}")
        got(f"t{slot}")
        ref[y, 0:rows] = ref[y, 0:rows] + yr2[slot, 0, 0:rows].astype(F32) + yr2[slot, 1, 0:rows].astype(F32)

    mine = pl.ds(pl.multiple_of(xl * 224, 32), 224)
    other = pl.ds(pl.multiple_of((1 - xl) * 224, 32), 224)

    def put_grad_one(slot, value):
        q = lax.rem(z + slot, 4)
        g1_o[:, :, lanes(q)] = value[0:216].reshape(27, 8, 128)

    def x_first(slot, lane):
        for n in range(4):
            xs4[lane, n] = acc[slot, n, other].astype(BF16)
        send(f"x{slot}", xs4.at[lane], xr4.at[lane], xpt)

    def x_second(slot, lane):
        got(f"x{slot}")
        for n in range(4):
            accx[lane, n] = acc[slot, n, mine] + xr4[lane, n].astype(F32)

    def x_last(slot, lane):
        xs1[lane] = acc[slot, y, other].astype(BF16)
        send(f"x{slot}", xs1.at[lane], xr1.at[lane], xpt)

    def x_done(slot, lane):
        got(f"x{slot}")
        put_grad_one(slot, acc[slot, y, mine] + xr1[lane].astype(F32))

    zm_rows, zp_rows = low, high

    grad_one(0)
    got("h1p")
    send("h2p", hid.at[zm_rows, lanes(zm)], hid.at[zm_rows, lanes(zm)], zup)
    got("h1m")
    send("h2m", hid.at[zp_rows, lanes(zp)], hid.at[zp_rows, lanes(zp)], zdn)
    add_sibling(0)
    y_first(0, acc.at[0], 448)
    got("d1p")
    send("d2p", dlt.at[zm_rows, lanes(zm)], dlt.at[zm_rows, lanes(zm)], zup)
    got("d1m")
    send("d2m", dlt.at[zp_rows, lanes(zp)], dlt.at[zp_rows, lanes(zp)], zdn)
    grad_one(1)
    add_sibling(1)
    x_first(1, 0)
    y_second(0, acc.at[0], 448)
    grad_one(3)
    add_sibling(3)
    x_first(3, 1)
    got("h2p")
    got("h2m")

    def turn_hidden(q, carry):
        flat = hid[:, lanes(q)].astype(F32).T.astype(BF16)
        for xd in range(2):
            for kd in range(2):
                j = xd * 2 + kd
                gh[kd, xd, q, xl * 2 + k] = flat[j * 32 : (j + 1) * 32]
        return carry

    lax.fori_loop(0, 4, turn_hidden, 0)
    src = xl * 2 + k
    send("g1", gh.at[1 - k, :, :, src], gh.at[1 - k, :, :, src], sib)
    x_second(1, 0)
    y_first(1, accx.at[0], 224)
    got("d2p")
    got("d2m")
    grad_one(2)
    y_third(0, acc.at[0], 448)
    x_last(0, 0)
    got("g1")
    pair_src = pl.ds(xl * 2, 2)
    send("g2", gh.at[k, 1 - xl, :, pair_src], gh.at[k, 1 - xl, :, pair_src], xpt)
    add_sibling(2)
    y_first(2, acc.at[2], 448)
    x_second(3, 1)
    y_first(3, accx.at[1], 224)
    y_second(1, accx.at[0], 224)

    fs[...] = jnp.zeros_like(fs)
    for later in range(2):
        for d in range(4):
            total = None
            for tap in range(27):
                do, di, dj = tap_shift(tap)
                if do != later or di * 2 + dj != d:
                    continue
                phase = tap_phase(tap)
                term = jnp.dot(
                    hid[phase * 64 : (phase + 1) * 64, :],
                    k2_v[tap * 512 : (tap + 1) * 512, :],
                    preferred_element_type=F32,
                )
                total = term if total is None else total + term
            fs[later, d, 1:9, 8:16, :] = total.reshape(8, 8, 256)
    for later in range(2):
        total = None
        for d in range(4):
            di, dj = d // 2, d % 2
            term = fs[later, d, 1 - di : 9 - di, 8 - dj : 16 - dj, :]
            total = term if total is None else total + term
        fp[later] = total.reshape(64, 256)
    send("f1", fp.at[1], fr, nxt)

    got("g2")
    hh[y] = gh[k, xl, y]
    send("g3p", gh.at[k, xl, yp], hh.at[y], yup)
    send("g3m", gh.at[k, xl, ym], hh.at[y], ydn)
    send("g3f", gh.at[k, xl, y2], hh.at[y], yfar)
    y_second(2, acc.at[2], 448)
    y_second(3, accx.at[1], 224)

    got("f1")
    whole = fp[0] + jnp.where(s > 0, fr[...], 0.0)
    for half in range(2):
        fx[half] = whole[:, half * 128 : (half + 1) * 128]
    send("f2", fx.at[1 - h], fxr, hpt)

    y_third(1, accx.at[0], 224)
    put_grad_one(1, accx[0, y])
    x_done(0, 0)

    got("g3p")
    got("g3m")
    got("g3f")
    for phase in range(8):
        for m in range(8):
            two_slabs = [hh[(2 * m + e) // 4, (2 * m + e) % 4, :, phase * 64 : (phase + 1) * 64] for e in range(2)]
            hp[phase * 32 : (phase + 1) * 32, m * 128 : (m + 1) * 128] = jnp.concatenate(two_slabs, 1)
    for do in range(2):
        for d in range(4):
            di, dj = d // 2, d % 2
            grads = jnp.dot(hp[...], up_s[d, do * 64 : do * 64 + 1024, :], preferred_element_type=F32)
            for tap in range(27):
                if tap_shift(tap) == (do, di, dj):
                    phase = tap_phase(tap)
                    g2_o[tap] = grads[phase * 32 : (phase + 1) * 32]

    y_third(2, acc.at[2], 448)
    x_last(2, 1)
    y_third(3, accx.at[1], 224)
    put_grad_one(3, accx[1, y])
    got("f2")
    feat_o[...] = fx[h] + fxr[...]
    x_done(2, 1)
    for message in msgs.values():
        message.wait_send()


def local(volume, kernel_one, kernel_two, upstream):
    any_spec = pl.BlockSpec(memory_space=pl.ANY)
    vmem_spec = pl.BlockSpec(memory_space=pltpu.VMEM)
    v = pltpu.VMEM
    feat, g1, g2 = pl.pallas_call(
        body,
        out_shape=(
            jax.ShapeDtypeStruct((64, 128), F32),
            jax.ShapeDtypeStruct((27, 8, 512), F32),
            jax.ShapeDtypeStruct((27, 32, 256), F32),
        ),
        in_specs=[any_spec] * 4,
        out_specs=(vmem_spec,) * 3,
        scratch_shapes=[
            v((4, 32, 32, 128), BF16),
            v((32, 32, 128), BF16),
            v((3456, 512), BF16),
            v((27 * 512, 256), BF16),
            v((5, 33, 40, 128), F32),
            v((512, 3456), BF16),
            v((16, 224, 512), BF16),
            v((2, 16, 64, 128), BF16),
            v((9, 16, 256), F32),
            v((4, 1088, 256), BF16),
            v((4, 512, 128), F32),
            v((2, 256, 128), F32),
            v((2, 512, 128), F32),
            v((4, 512, 128), F32),
            v((512, 128), BF16),
            v((2, 512, 128), BF16),
            v((2, 256, 128), BF16),
            v((2, 512, 128), BF16),
            v((512, 512), BF16),
            v((512, 512), BF16),
            v((4, 4, 448, 128), F32),
            v((4, 4, 448, 128), BF16),
            v((4, 4, 448, 128), BF16),
            v((2, 4, 224, 128), F32),
            v((2, 4, 224, 128), BF16),
            v((2, 4, 224, 128), BF16),
            v((2, 224, 128), BF16),
            v((2, 224, 128), BF16),
            v((4, 448, 128), BF16),
            v((4, 2, 224, 128), BF16),
            v((4, 2, 448, 128), BF16),
            v((4, 2, 448, 128), BF16),
            v((2, 2, 4, 4, 32, 512), BF16),
            v((4, 4, 32, 512), BF16),
            v((256, 1024), BF16),
            v((2, 4, 9, 16, 256), F32),
            v((2, 64, 256), F32),
            v((64, 256), F32),
            v((2, 64, 128), F32),
            v((64, 128), F32),
            pltpu.SemaphoreType.DMA((4,)),
            pltpu.SemaphoreType.DMA((NMSG,)),
            pltpu.SemaphoreType.DMA((NMSG,)),
        ],
        compiler_params=pltpu.CompilerParams(
            collective_id=0, has_side_effects=True, vmem_limit_bytes=60 * 1024 * 1024
        ),
        cost_estimate=pl.CostEstimate(flops=6_000_000_000, bytes_accessed=14_000_000, transcendentals=0),
        name="two_layers",
    )(
        volume,
        kernel_one.reshape(27 * 128, 512),
        kernel_two.reshape(27 * 512, 256),
        upstream.reshape(64, 128),
    )
    return feat.reshape(1, 8, 8, 128), g1, g2


def solution(mesh):
    return jax.shard_map(
        local,
        mesh=mesh,
        in_specs=(
            P("space", None, None, "chan"),
            P(None, "chan", "filt"),
            P(None, "filt", "chan"),
            P("space", None, None, ("chan", "filt")),
        ),
        out_specs=(
            P("space", None, None, ("chan", "filt")),
            P(None, ("chan", "space"), "filt"),
            P(None, ("filt", "space"), "chan"),
        ),
        check_vma=False,
    )
```

```python
import jax
import jax.numpy as jnp
from jax import lax
from jax.experimental import pallas as pl
from jax.experimental.pallas import tpu as pltpu
from jax.sharding import PartitionSpec as P

SLOPE = 0.3
F32, BF16 = jnp.float32, jnp.bfloat16
MESH = pl.DeviceIdType.MESH
NMSG = 80


def tap_parts(tap):
    return tap // 9, (tap // 3) % 3, tap % 3


def tap_phase(tap):
    a, b, c = tap_parts(tap)
    return ((a != 1) * 2 + (b != 1)) * 2 + (c != 1)


def tap_shift(tap):
    return tuple(int(v == 0) for v in tap_parts(tap))


def body(
    vol, k1, k2, up, feat_o, g1_o, g2_o,
    vol_v, halo_v, k1_v, k2_v, pf, patch, patch_t,
    up_all, up_next, up_f, up_s, seed_s,
    part, mr1, mr2, bpart, bs1, bs2, br1, br2,
    hid, dlt,
    acc, ksend, krecv, accx, xs4, xr4, xs1, xr1, ys1, yr1, ys2, yr2,
    gh, hh, hp, fs, fp, fr, fx, fxr, feat_v, g1_v, g2_v,
    lsem, ssem, rsem,
):
    s, z, h = lax.axis_index("space"), lax.axis_index("chan"), lax.axis_index("filt")
    k, pair = lax.rem(s, 2), lax.div(s, 2)
    xl, y = lax.rem(pair, 2), lax.div(pair, 2)
    zp, zm, z2 = lax.rem(z + 1, 4), lax.rem(z + 3, 4), lax.rem(z + 2, 4)
    yp, ym, y2 = lax.rem(y + 1, 4), lax.rem(y + 3, 4), lax.rem(y + 2, 4)
    around = [lax.rem(s + d, 16) for d in range(16)]
    sib = {"space": s + 1 - 2 * k}
    xpt = {"space": y * 4 + (1 - xl) * 2 + k}
    hpt = {"filt": 1 - h}
    yup, ydn, yfar = ({"space": v * 4 + xl * 2 + k} for v in (yp, ym, y2))
    zup, zdn, zfar = {"chan": zp}, {"chan": zm}, {"chan": z2}
    nxt, prv = {"space": around[1]}, {"space": around[15]}
    nxt_h, prv_h = {"space": around[1], "filt": 1 - h}, {"space": around[15], "filt": 1 - h}

    msgs = {}

    def send(name, src, dst, device):
        i = len(msgs)
        msgs[name] = pltpu.make_async_remote_copy(
            src_ref=src, dst_ref=dst, send_sem=ssem.at[i], recv_sem=rsem.at[i], device_id=device, device_id_type=MESH
        )
        msgs[name].start()

    def got(name):
        msgs[name].wait_recv()

    def lanes(q):
        return pl.ds(pl.multiple_of(q * 128, 128), 128)

    loads = [
        pltpu.make_async_copy(vol, vol_v, lsem.at[0]),
        pltpu.make_async_copy(up, up_all.at[h, s], lsem.at[1]),
        pltpu.make_async_copy(k1, k1_v, lsem.at[2]),
        pltpu.make_async_copy(k2, k2_v, lsem.at[3]),
    ]
    for copy in loads:
        copy.start()

    barrier = pltpu.get_barrier_semaphore()
    greeted = [{"space": v} for v in around[1:]] + [zup, zdn, zfar, hpt, nxt_h, prv_h]
    for device in greeted:
        pl.semaphore_signal(barrier, inc=1, device_id=device, device_id_type=MESH)
    pl.semaphore_wait(barrier, len(greeted))

    send("halo", vol.at[3], halo_v, nxt)
    loads[1].wait()
    send("u0", up_all.at[h, s], up_all.at[h, s], hpt)
    send("u1", up_all.at[h, s], up_next.at[h], prv)
    send("u2", up_all.at[h, s], up_next.at[h], prv_h)

    zero_row = jnp.zeros((40, 128), F32)
    zero_col = jnp.zeros((33, 8, 128), F32)
    for p in range(5):
        pf[p, 0] = zero_row
        pf[p, :, 0:8, :] = zero_col
    loads[0].wait()

    def widen(r, carry):
        for p in range(4):
            pf[p + 1, r + 1, 8:40, :] = vol_v[p, r].astype(F32)
        return carry

    lax.fori_loop(0, 32, widen, 0)

    def build(o, depth_taps):
        def step(n, carry):
            pi, ii = lax.div(n, 4), lax.rem(n, 4)
            for pj in range(2):
                base = pl.multiple_of((o * 4 + pi * 2 + pj) * 64 + ii * 16, 16)
                for a in depth_taps:
                    for b in range(3):
                        row = 8 * ii + 2 * pi + b
                        for c in range(3):
                            tap = 9 * a + 3 * b + c
                            cols = pl.ds(7 + 2 * pj + c, 8, stride=4)
                            both = [pf[2 * o + a, row + 4 * e, cols, :] for e in range(2)]
                            patch[pl.ds(base, 16), tap * 128 : (tap + 1) * 128] = jnp.concatenate(both, 0).astype(BF16)
            return carry

        lax.fori_loop(0, 8, step, 0)

    build(1, (0, 1, 2))
    loads[2].wait()
    low, high = pl.ds(0, 256), pl.ds(256, 256)

    def conv_one(first, second, rows):
        weights = jnp.concatenate([k1_v[:, lanes(lax.rem(z + away, 4))] for away in (first, second)], 1)
        both = jnp.dot(patch[rows, :], weights, preferred_element_type=F32)
        part[first, rows, :] = both[:, 0:128]
        part[second, rows, :] = both[:, 128:256]

    conv_one(2, 1, high)
    send("m1m", part.at[2, high], mr1.at[1], zdn)
    send("m2pb", part.at[1, high], mr2.at[0, high], zup)
    conv_one(3, 0, high)

    up_f[...] = jnp.zeros_like(up_f)

    def moved(blocks, store):
        for half in range(2):
            up_f[0:8, 0:8, half * 128 : (half + 1) * 128] = blocks[half].astype(F32).reshape(8, 8, 128)
        for di in range(2):
            for dj in range(2):
                store(di * 2 + dj, up_f[di : di + 8, dj : dj + 8, :].reshape(64, 256).astype(BF16))

    got("u0")
    got("u1")
    got("u2")
    own_pair = up_all.at[:, s]
    for d in range(1, 16):
        send(f"a{d}", own_pair, own_pair, {"space": around[d]})

    def store_seed(later):
        def store(d, value):
            seed_s[later, d] = value

        return store

    moved([up_all[half, s] for half in range(2)], store_seed(0))
    moved([jnp.where(s < 15, up_next[half].astype(F32), 0.0) for half in range(2)], store_seed(1))

    loads[3].wait()
    for phase in range(8):
        total = None
        for tap in range(27):
            if tap_phase(tap) != phase:
                continue
            do, di, dj = tap_shift(tap)
            term = lax.dot_general(
                seed_s[do, di * 2 + dj],
                k2_v[tap * 512 : (tap + 1) * 512, :],
                (((1,), (1,)), ((), ())),
                preferred_element_type=F32,
            )
            total = term if total is None else total + term
        for q in range(4):
            bpart[q, phase * 64 : (phase + 1) * 64, :] = total[:, q * 128 : (q + 1) * 128]
    bs1[...] = bpart[z2].astype(BF16)
    send("b1p", bs1.at[low], br1.at[0], zup)
    send("b1m", bs1.at[high], br1.at[1], zdn)
    bs2[0, 256:512] = bpart[zp, 256:512].astype(BF16)
    send("b2pb", bs2.at[0, high], br2.at[0, high], zup)
    bs2[1, 0:256] = bpart[zm, 0:256].astype(BF16)
    send("b2ma", bs2.at[1, low], br2.at[1, low], zdn)

    build(0, (1, 2))
    got("halo")

    def widen_halo(r, carry):
        pf[0, r + 1, 8:40, :] = jnp.where(s > 0, halo_v[r].astype(F32), 0.0)
        return carry

    lax.fori_loop(0, 32, widen_halo, 0)
    build(0, (0,))
    conv_one(2, 3, low)
    send("m1p", part.at[2, low], mr1.at[0], zup)
    send("m2ma", part.at[3, low], mr2.at[1, low], zdn)
    got("m1m")
    part[3, 256:512] += mr1[1]
    send("m2mb", part.at[3, high], mr2.at[1, high], zdn)
    conv_one(1, 0, low)
    got("m1p")
    part[1, 0:256] += mr1[0]
    send("m2pa", part.at[1, low], mr2.at[0, low], zup)
    got("b1p")
    bs2[0, 0:256] = (bpart[zp, 0:256] + br1[0].astype(F32)).astype(BF16)
    send("b2pa", bs2.at[0, low], br2.at[0, low], zup)
    got("b1m")
    bs2[1, 256:512] = (bpart[zm, 256:512] + br1[1].astype(F32)).astype(BF16)
    send("b2mb", bs2.at[1, high], br2.at[1, high], zdn)

    def put_turned(flat_rows, rows_at):
        for owner in range(16):
            yd, xd, kd = owner // 4, (owner // 2) % 2, owner % 2
            patch_t[kd, yd, pl.ds(pl.multiple_of(rows_at + xd * 224, 16), 16), :] = flat_rows(owner).astype(BF16)

    def turn(n, carry):
        flat = patch[:, pl.ds(pl.multiple_of(n * 256, 256), 256)].astype(F32).T

        def two_taps(owner):
            return jnp.concatenate([flat[e * 128 + owner * 8 : e * 128 + owner * 8 + 8] for e in range(2)], 0)

        put_turned(two_taps, n * 16)
        return carry

    lax.fori_loop(0, 13, turn, 0)
    flat = patch[:, 26 * 128 : 27 * 128].astype(F32).T
    put_turned(lambda owner: jnp.concatenate([flat[owner * 8 : owner * 8 + 8], jnp.zeros((8, 512), F32)], 0), 208)

    for d in range(4):
        up_s[d, 1024:1088, :] = jnp.zeros((64, 256), BF16)
    for d in range(1, 16):
        got(f"a{d}")

    def shifted(slab, carry):
        def store(d, value):
            up_s[d, pl.ds(pl.multiple_of(slab * 64, 64), 64), :] = value

        moved([up_all[half, slab] for half in range(2)], store)
        return carry

    lax.fori_loop(0, 16, shifted, 0)

    for name in ("m2pb", "m2ma", "m2pa", "m2mb"):
        got(name)
    mixed = part[0] + mr2[0] + mr2[1]
    part[0] = mixed
    hid[:, lanes(z)] = jnp.where(mixed > 0, mixed, SLOPE * mixed).astype(BF16)
    for name in ("b2pb", "b2ma", "b2pa", "b2mb"):
        got(name)
    back = bpart[z] + br2[0].astype(F32) + br2[1].astype(F32)
    dlt[:, lanes(z)] = (back * jnp.where(part[0] > 0, 1.0, SLOPE)).astype(BF16)
    for tag, ref in (("d", dlt), ("h", hid)):
        for way, device in (("p", zup), ("m", zdn), ("f", zfar)):
            send(tag + way, ref.at[:, lanes(z)], ref.at[:, lanes(z)], device)

    def grad_one(slots):
        deltas = jnp.concatenate([dlt[:, lanes(lax.rem(z + slot, 4))] for slot in slots], 1)
        for yd in range(4):
            term = jnp.dot(patch_t[1 - k, yd], deltas, preferred_element_type=F32)
            for i, slot in enumerate(slots):
                ksend[slot, yd] = term[:, i * 128 : (i + 1) * 128].astype(BF16)
        for slot in slots:
            send(f"k{slot}", ksend.at[slot], krecv.at[slot], sib)
        for yd in range(4):
            term = jnp.dot(patch_t[k, yd], deltas, preferred_element_type=F32)
            for i, slot in enumerate(slots):
                acc[slot, yd] = term[:, i * 128 : (i + 1) * 128]

    def add_sibling(slot):
        got(f"k{slot}")

        def step(n, carry):
            acc[slot, n] += krecv[slot, n].astype(F32)
            return carry

        lax.fori_loop(0, 4, step, 0)

    def ring_first(slot, ref, rows):
        half = rows // 2
        ys1[0:rows] = ref[y2].astype(BF16)
        send(f"p{slot}", ys1.at[0:half], yr1.at[0, 0:half], yup)
        send(f"q{slot}", ys1.at[half:rows], yr1.at[1, 0:half], ydn)

    def ring_second(slot, ref, rows):
        half = rows // 2
        got(f"p{slot}")
        ys2[slot, 0, 0:half] = (ref[yp, 0:half] + yr1[0, 0:half].astype(F32)).astype(BF16)
        ys2[slot, 0, half:rows] = ref[yp, half:rows].astype(BF16)
        send(f"r{slot}", ys2.at[slot, 0, 0:rows], yr2.at[slot, 0, 0:rows], yup)
        got(f"q{slot}")
        ys2[slot, 1, 0:half] = ref[ym, 0:half].astype(BF16)
        ys2[slot, 1, half:rows] = (ref[ym, half:rows] + yr1[1, 0:half].astype(F32)).astype(BF16)
        send(f"t{slot}", ys2.at[slot, 1, 0:rows], yr2.at[slot, 1, 0:rows], ydn)

    def ring_third(slot, ref, rows):
        got(f"r{slot}")
        got(f"t{slot}")
        ref[y, 0:rows] = ref[y, 0:rows] + yr2[slot, 0, 0:rows].astype(F32) + yr2[slot, 1, 0:rows].astype(F32)

    def straight(slot, ref, rows):
        for i, (v, device) in enumerate(((y2, yfar), (yp, yup), (ym, ydn))):
            ys2[slot, i, 0:rows] = ref[v].astype(BF16)
            send(f"y{slot}{i}", ys2.at[slot, i, 0:rows], yr2.at[slot, i, 0:rows], device)

    def straight_sum(slot, ref, rows):
        for i in (1, 2, 0):
            got(f"y{slot}{i}")
        total = ref[y, 0:rows]
        for i in range(3):
            total = total + yr2[slot, i, 0:rows].astype(F32)
        ref[y, 0:rows] = total

    mine = pl.ds(pl.multiple_of(xl * 224, 32), 224)
    other = pl.ds(pl.multiple_of((1 - xl) * 224, 32), 224)

    def put_grad_one(slot, value):
        q = lax.rem(z + slot, 4)
        g1_v[:, :, lanes(q)] = value[0:216].reshape(27, 8, 128)

    def x_first(slot, lane):
        for n in range(4):
            xs4[lane, n] = acc[slot, n, other].astype(BF16)
        send(f"x{slot}", xs4.at[lane], xr4.at[lane], xpt)

    def x_second(slot, lane):
        got(f"x{slot}")
        for n in range(4):
            accx[lane, n] = acc[slot, n, mine] + xr4[lane, n].astype(F32)

    def x_last(slot, lane):
        xs1[lane] = acc[slot, y, other].astype(BF16)
        send(f"x{slot}", xs1.at[lane], xr1.at[lane], xpt)

    def x_done(slot, lane):
        got(f"x{slot}")
        put_grad_one(slot, acc[slot, y, mine] + xr1[lane].astype(F32))

    grad_one((0,))
    add_sibling(0)
    ring_first(0, acc.at[0], 448)
    got("dp")
    got("dm")
    grad_one((1, 3))
    ring_second(0, acc.at[0], 448)
    add_sibling(1)
    x_first(1, 0)
    add_sibling(3)
    x_first(3, 1)
    got("df")
    grad_one((2,))
    add_sibling(2)
    straight(2, acc.at[2], 448)
    ring_third(0, acc.at[0], 448)
    x_last(0, 0)
    x_second(1, 0)
    straight(1, accx.at[0], 224)
    x_second(3, 1)
    straight(3, accx.at[1], 224)
    for way in "pmf":
        got("h" + way)

    def turn_hidden(q, carry):
        flat = hid[:, lanes(q)].astype(F32).T.astype(BF16)
        for j in range(4):
            gh[q * 4 + j] = flat[j * 32 : (j + 1) * 32]
        return carry

    lax.fori_loop(0, 4, turn_hidden, 0)
    for d in range(1, 16):
        send(f"g{d}", gh.at[around[d]], hh.at[s], {"space": around[d]})
    hh[s] = gh[s]

    fs[...] = jnp.zeros_like(fs)
    for later in range(2):
        for d in range(4):
            total = None
            for tap in range(27):
                do, di, dj = tap_shift(tap)
                if do != later or di * 2 + dj != d:
                    continue
                phase = tap_phase(tap)
                term = jnp.dot(
                    hid[phase * 64 : (phase + 1) * 64, :],
                    k2_v[tap * 512 : (tap + 1) * 512, :],
                    preferred_element_type=F32,
                )
                total = term if total is None else total + term
            fs[later, d, 1:9, 8:16, :] = total.reshape(8, 8, 256)
    for later in range(2):
        total = None
        for d in range(4):
            di, dj = d // 2, d % 2
            term = fs[later, d, 1 - di : 9 - di, 8 - dj : 16 - dj, :]
            total = term if total is None else total + term
        fp[later] = total.reshape(64, 256)
    send("f1", fp.at[1], fr, nxt)

    straight_sum(2, acc.at[2], 448)
    x_last(2, 1)
    got("f1")
    whole = fp[0] + jnp.where(s > 0, fr[...], 0.0)
    for half in range(2):
        fx[half] = whole[:, half * 128 : (half + 1) * 128]
    send("f2", fx.at[1 - h], fxr, hpt)
    straight_sum(1, accx.at[0], 224)
    put_grad_one(1, accx[0, y])
    straight_sum(3, accx.at[1], 224)
    put_grad_one(3, accx[1, y])
    x_done(0, 0)

    for d in range(1, 16):
        got(f"g{d}")
    for phase in range(8):
        for m in range(8):
            two_slabs = [hh[2 * m + e, :, phase * 64 : (phase + 1) * 64] for e in range(2)]
            hp[phase * 32 : (phase + 1) * 32, m * 128 : (m + 1) * 128] = jnp.concatenate(two_slabs, 1)
    for do in range(2):
        for d in range(4):
            di, dj = d // 2, d % 2
            grads = jnp.dot(hp[...], up_s[d, do * 64 : do * 64 + 1024, :], preferred_element_type=F32)
            for tap in range(27):
                if tap_shift(tap) == (do, di, dj):
                    phase = tap_phase(tap)
                    g2_v[tap] = grads[phase * 32 : (phase + 1) * 32]
    stores = [pltpu.make_async_copy(g2_v, g2_o, lsem.at[4])]
    stores[0].start()
    x_done(2, 1)
    stores.append(pltpu.make_async_copy(g1_v, g1_o, lsem.at[5]))
    stores[1].start()
    got("f2")
    feat_v[...] = fx[h] + fxr[...]
    stores.append(pltpu.make_async_copy(feat_v, feat_o, lsem.at[6]))
    stores[2].start()
    for message in msgs.values():
        message.wait_send()
    for copy in stores:
        copy.wait()


def place(feat, g1, g2, feat_o, g1_o, g2_o):
    feat_o[...] = feat[...]
    g1_o[...] = g1[...]
    g2_o[...] = g2[...]


def local(volume, kernel_one, kernel_two, upstream):
    any_spec = pl.BlockSpec(memory_space=pl.ANY)
    v = pltpu.VMEM
    shapes = (
        jax.ShapeDtypeStruct((64, 128), F32),
        jax.ShapeDtypeStruct((27, 8, 512), F32),
        jax.ShapeDtypeStruct((27, 32, 256), F32),
    )
    place_specs = (
        pl.BlockSpec((64, 128), lambda i: (0, 0)),
        pl.BlockSpec((9, 8, 512), lambda i: (i, 0, 0)),
        pl.BlockSpec((9, 32, 256), lambda i: (i, 0, 0)),
    )
    results = pl.pallas_call(
        body,
        out_shape=shapes,
        in_specs=[any_spec] * 4,
        out_specs=(any_spec,) * 3,
        scratch_shapes=[
            v((4, 32, 32, 128), BF16),
            v((32, 32, 128), BF16),
            v((3456, 512), BF16),
            v((27 * 512, 256), BF16),
            v((5, 33, 40, 128), F32),
            v((512, 3456), BF16),
            v((2, 4, 448, 512), BF16),
            v((2, 16, 64, 128), BF16),
            v((2, 64, 128), BF16),
            v((9, 16, 256), F32),
            v((4, 1088, 256), BF16),
            v((2, 4, 64, 256), BF16),
            v((4, 512, 128), F32),
            v((2, 256, 128), F32),
            v((2, 512, 128), F32),
            v((4, 512, 128), F32),
            v((512, 128), BF16),
            v((2, 512, 128), BF16),
            v((2, 256, 128), BF16),
            v((2, 512, 128), BF16),
            v((512, 512), BF16),
            v((512, 512), BF16),
            v((4, 4, 448, 128), F32),
            v((4, 4, 448, 128), BF16),
            v((4, 4, 448, 128), BF16),
            v((2, 4, 224, 128), F32),
            v((2, 4, 224, 128), BF16),
            v((2, 4, 224, 128), BF16),
            v((2, 224, 128), BF16),
            v((2, 224, 128), BF16),
            v((448, 128), BF16),
            v((2, 224, 128), BF16),
            v((4, 3, 448, 128), BF16),
            v((4, 3, 448, 128), BF16),
            v((16, 32, 512), BF16),
            v((16, 32, 512), BF16),
            v((256, 1024), BF16),
            v((2, 4, 9, 16, 256), F32),
            v((2, 64, 256), F32),
            v((64, 256), F32),
            v((2, 64, 128), F32),
            v((64, 128), F32),
            v((64, 128), F32),
            v((27, 8, 512), F32),
            v((27, 32, 256), F32),
            pltpu.SemaphoreType.DMA((7,)),
            pltpu.SemaphoreType.DMA((NMSG,)),
            pltpu.SemaphoreType.DMA((NMSG,)),
        ],
        compiler_params=pltpu.CompilerParams(
            collective_id=0, has_side_effects=True, vmem_limit_bytes=60 * 1024 * 1024
        ),
        cost_estimate=pl.CostEstimate(flops=6_000_000_000, bytes_accessed=14_000_000, transcendentals=0),
        name="two_layers",
    )(
        volume,
        kernel_one.reshape(27 * 128, 512),
        kernel_two.reshape(27 * 512, 256),
        upstream.reshape(64, 128),
    )
    feat, g1, g2 = pl.pallas_call(
        place,
        out_shape=shapes,
        grid=(3,),
        in_specs=place_specs,
        out_specs=place_specs,
        name="place",
    )(*results)
    return feat.reshape(1, 8, 8, 128), g1, g2


def solution(mesh):
    return jax.shard_map(
        local,
        mesh=mesh,
        in_specs=(
            P("space", None, None, "chan"),
            P(None, "chan", "filt"),
            P(None, "filt", "chan"),
            P("space", None, None, ("chan", "filt")),
        ),
        out_specs=(
            P("space", None, None, ("chan", "filt")),
            P(None, ("chan", "space"), "filt"),
            P(None, ("filt", "space"), "chan"),
        ),
        check_vma=False,
    )
```

```python
import jax
import jax.numpy as jnp
from jax import lax
from jax.experimental import pallas as pl
from jax.experimental.pallas import tpu as pltpu
from jax.sharding import PartitionSpec as P

SLOPE = 0.3
F32, BF16 = jnp.float32, jnp.bfloat16
MESH = pl.DeviceIdType.MESH
NMSG = 96


def tap_parts(tap):
    return tap // 9, (tap // 3) % 3, tap % 3


def tap_phase(tap):
    a, b, c = tap_parts(tap)
    return ((a != 1) * 2 + (b != 1)) * 2 + (c != 1)


def tap_shift(tap):
    return tuple(int(v == 0) for v in tap_parts(tap))


def body(
    vol, k1, k2, up, feat_o, g1_o, g2_o,
    vol_v, halo_v, k1_v, k2_v, pf, patch, patch_t,
    up_all, up_next, up_f, up_s, seed_s,
    part, mr1, mrf, mr2, bpart, bs1, bs2, br1, br2,
    hid, dlt,
    acc, ksend, krecv, accx, xs4, xr4, xs1, xr1, half_sum, ys1, yr1, ys2, yr2,
    gh, hh, hp, fs, fp, fr, fx, fxr, feat_v, g1_v, g2_v,
    lsem, ssem, rsem,
):
    s, z, h = lax.axis_index("space"), lax.axis_index("chan"), lax.axis_index("filt")
    k, pair = lax.rem(s, 2), lax.div(s, 2)
    xl, y = lax.rem(pair, 2), lax.div(pair, 2)
    zp, zm, z2 = lax.rem(z + 1, 4), lax.rem(z + 3, 4), lax.rem(z + 2, 4)
    yp, ym, y2 = lax.rem(y + 1, 4), lax.rem(y + 3, 4), lax.rem(y + 2, 4)
    around = [lax.rem(s + d, 16) for d in range(16)]
    sib = {"space": s + 1 - 2 * k}
    xpt = {"space": y * 4 + (1 - xl) * 2 + k}
    hpt = {"filt": 1 - h}
    yup, ydn, yfar = ({"space": v * 4 + xl * 2 + k} for v in (yp, ym, y2))
    zup, zdn, zfar = {"chan": zp}, {"chan": zm}, {"chan": z2}
    nxt, prv = {"space": around[1]}, {"space": around[15]}
    nxt_h, prv_h = {"space": around[1], "filt": 1 - h}, {"space": around[15], "filt": 1 - h}

    msgs = {}

    def send(name, src, dst, device):
        i = len(msgs)
        msgs[name] = pltpu.make_async_remote_copy(
            src_ref=src, dst_ref=dst, send_sem=ssem.at[i], recv_sem=rsem.at[i], device_id=device, device_id_type=MESH
        )
        msgs[name].start()

    def got(name):
        msgs[name].wait_recv()

    def lanes(q):
        return pl.ds(pl.multiple_of(q * 128, 128), 128)

    loads = [
        pltpu.make_async_copy(vol, vol_v, lsem.at[0]),
        pltpu.make_async_copy(up, up_all.at[h, s], lsem.at[1]),
        pltpu.make_async_copy(k1, k1_v, lsem.at[2]),
        pltpu.make_async_copy(k2, k2_v, lsem.at[3]),
    ]
    for copy in loads[0:3]:
        copy.start()

    barrier = pltpu.get_barrier_semaphore()
    greeted = [{"space": v} for v in around[1:]] + [zup, zdn, zfar, hpt, nxt_h, prv_h]
    for device in greeted:
        pl.semaphore_signal(barrier, inc=1, device_id=device, device_id_type=MESH)
    pl.semaphore_wait(barrier, len(greeted))

    loads[1].wait()
    send("u0", up_all.at[h, s], up_all.at[h, s], hpt)
    send("u1", up_all.at[h, s], up_next.at[h], prv)
    send("u2", up_all.at[h, s], up_next.at[h], prv_h)
    loads[0].wait()
    send("halo", vol_v.at[3], halo_v, nxt)
    loads[3].start()

    zero_row = jnp.zeros((40, 128), F32)
    zero_col = jnp.zeros((33, 8, 128), F32)
    for p in range(5):
        pf[p, 0] = zero_row
        pf[p, :, 0:8, :] = zero_col

    def widen(r, carry):
        for p in range(4):
            pf[p + 1, r + 1, 8:40, :] = vol_v[p, r].astype(F32)
        return carry

    lax.fori_loop(0, 32, widen, 0)

    def build(o, depth_taps):
        def step(n, carry):
            pi, ii = lax.div(n, 4), lax.rem(n, 4)
            for pj in range(2):
                base = pl.multiple_of((o * 4 + pi * 2 + pj) * 64 + ii * 16, 16)
                for a in depth_taps:
                    for b in range(3):
                        row = 8 * ii + 2 * pi + b
                        for c in range(3):
                            tap = 9 * a + 3 * b + c
                            cols = pl.ds(7 + 2 * pj + c, 8, stride=4)
                            both = [pf[2 * o + a, row + 4 * e, cols, :] for e in range(2)]
                            patch[pl.ds(base, 16), tap * 128 : (tap + 1) * 128] = jnp.concatenate(both, 0).astype(BF16)
            return carry

        lax.fori_loop(0, 8, step, 0)

    build(1, (0, 1, 2))
    loads[2].wait()
    low, high = pl.ds(0, 256), pl.ds(256, 256)

    def conv_one(first, second, rows):
        weights = jnp.concatenate([k1_v[:, lanes(lax.rem(z + away, 4))] for away in (first, second)], 1)
        both = jnp.dot(patch[rows, :], weights, preferred_element_type=F32)
        part[first, rows, :] = both[:, 0:128]
        part[second, rows, :] = both[:, 128:256]

    conv_one(2, 1, high)
    send("m1m", part.at[2, high], mr1, zdn)
    send("m2pb", part.at[1, high], mr2.at[0, high], zup)
    conv_one(3, 0, high)
    build(0, (1, 2))

    up_f[...] = jnp.zeros_like(up_f)

    def moved(blocks, store):
        for half in range(2):
            up_f[0:8, 0:8, half * 128 : (half + 1) * 128] = blocks[half].astype(F32).reshape(8, 8, 128)
        for di in range(2):
            for dj in range(2):
                store(di * 2 + dj, up_f[di : di + 8, dj : dj + 8, :].reshape(64, 256).astype(BF16))

    got("u0")
    got("u1")
    got("u2")
    def store_seed(later):
        def store(d, value):
            seed_s[later, d] = value

        return store

    moved([up_all[half, s] for half in range(2)], store_seed(0))
    moved([jnp.where(s < 15, up_next[half].astype(F32), 0.0) for half in range(2)], store_seed(1))

    loads[3].wait()
    for phase in range(8):
        total = None
        for tap in range(27):
            if tap_phase(tap) != phase:
                continue
            do, di, dj = tap_shift(tap)
            term = lax.dot_general(
                seed_s[do, di * 2 + dj],
                k2_v[tap * 512 : (tap + 1) * 512, :],
                (((1,), (1,)), ((), ())),
                preferred_element_type=F32,
            )
            total = term if total is None else total + term
        for q in range(4):
            bpart[q, phase * 64 : (phase + 1) * 64, :] = total[:, q * 128 : (q + 1) * 128]
    bs1[...] = bpart[z2].astype(BF16)
    send("b1p", bs1.at[low], br1.at[0], zup)
    send("b1m", bs1.at[high], br1.at[1], zdn)
    bs2[0, 256:512] = bpart[zp, 256:512].astype(BF16)
    send("b2pb", bs2.at[0, high], br2.at[0, high], zup)
    bs2[1, 0:256] = bpart[zm, 0:256].astype(BF16)
    send("b2ma", bs2.at[1, low], br2.at[1, low], zdn)

    got("halo")

    def widen_halo(r, carry):
        pf[0, r + 1, 8:40, :] = jnp.where(s > 0, halo_v[r].astype(F32), 0.0)
        return carry

    lax.fori_loop(0, 32, widen_halo, 0)
    build(0, (0,))
    conv_one(2, 3, low)
    send("m1p", part.at[2, low], mrf, zup)
    send("m2ma", part.at[3, low], mr2.at[1, low], zdn)
    own_pair = up_all.at[:, s]
    for d in range(1, 16):
        send(f"a{d}", own_pair, own_pair, {"space": around[d]})
    got("m1m")
    part[3, 256:512] += mr1[...]
    send("m2mb", part.at[3, high], mr2.at[1, high], zdn)
    conv_one(1, 0, low)
    got("b1p")
    bs2[0, 0:256] = (bpart[zp, 0:256] + br1[0].astype(F32)).astype(BF16)
    send("b2pa", bs2.at[0, low], br2.at[0, low], zup)
    got("b1m")
    bs2[1, 256:512] = (bpart[zm, 256:512] + br1[1].astype(F32)).astype(BF16)
    send("b2mb", bs2.at[1, high], br2.at[1, high], zdn)
    got("m1p")
    part[1, 0:256] += mrf[...]
    send("m2pa", part.at[1, low], mr2.at[0, low], zup)

    def put_turned(flat_rows, rows_at):
        for owner in range(16):
            yd, xd, kd = owner // 4, (owner // 2) % 2, owner % 2
            patch_t[kd, yd, pl.ds(pl.multiple_of(rows_at + xd * 224, 16), 16), :] = flat_rows(owner).astype(BF16)

    def turn(n, carry):
        flat = patch[:, pl.ds(pl.multiple_of(n * 256, 256), 256)].astype(F32).T

        def two_taps(owner):
            return jnp.concatenate([flat[e * 128 + owner * 8 : e * 128 + owner * 8 + 8] for e in range(2)], 0)

        put_turned(two_taps, n * 16)
        return carry

    lax.fori_loop(0, 13, turn, 0)
    flat = patch[:, 26 * 128 : 27 * 128].astype(F32).T
    put_turned(lambda owner: jnp.concatenate([flat[owner * 8 : owner * 8 + 8], jnp.zeros((8, 512), F32)], 0), 208)

    for d in range(4):
        up_s[d, 1024:1088, :] = jnp.zeros((64, 256), BF16)
    for d in range(1, 16):
        got(f"a{d}")

    def shifted(slab, carry):
        def store(d, value):
            up_s[d, pl.ds(pl.multiple_of(slab * 64, 64), 64), :] = value

        moved([up_all[half, slab] for half in range(2)], store)
        return carry

    lax.fori_loop(0, 16, shifted, 0)

    for name in ("m2pb", "m2ma", "m2mb", "m2pa"):
        got(name)
    mixed = part[0] + mr2[0] + mr2[1]
    part[0] = mixed
    hid[:, lanes(z)] = jnp.where(mixed > 0, mixed, SLOPE * mixed).astype(BF16)
    ways = (("p", zup, zp), ("m", zdn, zm), ("f", zfar, z2))

    def quarter(v):
        return hid.at[pl.ds(pl.multiple_of(v * 128, 128), 128), lanes(z)]

    for way, device, v in ways:
        send("e" + way, quarter(v), quarter(v), device)
    for name in ("b2pb", "b2ma", "b2pa", "b2mb"):
        got(name)
    back = bpart[z] + br2[0].astype(F32) + br2[1].astype(F32)
    dlt[:, lanes(z)] = (back * jnp.where(part[0] > 0, 1.0, SLOPE)).astype(BF16)
    own_delta = dlt.at[:, lanes(z)]
    send("dp", own_delta, own_delta, zup)
    send("dm", own_delta, own_delta, zdn)

    def grad_one(slots):
        deltas = jnp.concatenate([dlt[:, lanes(lax.rem(z + slot, 4))] for slot in slots], 1)
        for yd in range(4):
            term = jnp.dot(patch_t[1 - k, yd], deltas, preferred_element_type=F32)
            for i, slot in enumerate(slots):
                ksend[slot, yd] = term[:, i * 128 : (i + 1) * 128].astype(BF16)
        for slot in slots:
            send(f"k{slot}", ksend.at[slot], krecv.at[slot], sib)
        for yd in range(4):
            term = jnp.dot(patch_t[k, yd], deltas, preferred_element_type=F32)
            for i, slot in enumerate(slots):
                acc[slot, yd] = term[:, i * 128 : (i + 1) * 128]

    def add_sibling(slot):
        got(f"k{slot}")

        def step(n, carry):
            acc[slot, n] += krecv[slot, n].astype(F32)
            return carry

        lax.fori_loop(0, 4, step, 0)

    def ring_first(slot, ref, rows):
        half = rows // 2
        ys1[0:rows] = ref[y2].astype(BF16)
        send(f"p{slot}", ys1.at[0:half], yr1.at[0, 0:half], yup)
        send(f"q{slot}", ys1.at[half:rows], yr1.at[1, 0:half], ydn)

    def ring_second(slot, ref, rows):
        half = rows // 2
        got(f"p{slot}")
        ys2[slot, 0, 0:half] = (ref[yp, 0:half] + yr1[0, 0:half].astype(F32)).astype(BF16)
        ys2[slot, 0, half:rows] = ref[yp, half:rows].astype(BF16)
        send(f"r{slot}", ys2.at[slot, 0, 0:rows], yr2.at[slot, 0, 0:rows], yup)
        got(f"q{slot}")
        ys2[slot, 1, 0:half] = ref[ym, 0:half].astype(BF16)
        ys2[slot, 1, half:rows] = (ref[ym, half:rows] + yr1[1, 0:half].astype(F32)).astype(BF16)
        send(f"t{slot}", ys2.at[slot, 1, 0:rows], yr2.at[slot, 1, 0:rows], ydn)

    def ring_third(slot, ref, rows):
        got(f"r{slot}")
        got(f"t{slot}")
        ref[y, 0:rows] = ref[y, 0:rows] + yr2[slot, 0, 0:rows].astype(F32) + yr2[slot, 1, 0:rows].astype(F32)

    def straight(slot, ref, rows):
        for i, (v, device) in enumerate(((y2, yfar), (yp, yup), (ym, ydn))):
            ys2[slot, i, 0:rows] = ref[v].astype(BF16)
            send(f"y{slot}{i}", ys2.at[slot, i, 0:rows], yr2.at[slot, i, 0:rows], device)

    def straight_sum(slot, ref, rows):
        for i in (1, 2, 0):
            got(f"y{slot}{i}")
        total = ref[y, 0:rows]
        for i in range(3):
            total = total + yr2[slot, i, 0:rows].astype(F32)
        ref[y, 0:rows] = total

    mine = pl.ds(pl.multiple_of(xl * 224, 32), 224)
    other = pl.ds(pl.multiple_of((1 - xl) * 224, 32), 224)

    def put_grad_one(slot, value, first=0, last=27):
        q = lax.rem(z + slot, 4)
        g1_v[first:last, :, lanes(q)] = value[0 : (last - first) * 8].reshape(last - first, 8, 128)

    def x_first(slot, lane):
        for n in range(4):
            xs4[lane, n] = acc[slot, n, other].astype(BF16)
        send(f"x{slot}", xs4.at[lane], xr4.at[lane], xpt)

    def x_second(slot, lane):
        got(f"x{slot}")
        for n in range(4):
            accx[lane, n] = acc[slot, n, mine] + xr4[lane, n].astype(F32)

    def x_last(slot, lane):
        xs1[lane] = acc[slot, y, other].astype(BF16)
        send(f"x{slot}", xs1.at[lane], xr1.at[lane], xpt)

    def x_done(slot, lane):
        got(f"x{slot}")
        put_grad_one(slot, acc[slot, y, mine] + xr1[lane].astype(F32))

    def halved(v):
        return jnp.concatenate([acc[2, v, 0:112], acc[2, v, 224:336]], 0)

    def half_y():
        for i, (v, device) in enumerate(((y2, yfar), (yp, yup), (ym, ydn))):
            ys2[2, i, 0:224] = halved(v).astype(BF16)
            send(f"y2{i}", ys2.at[2, i, 0:224], yr2.at[2, i, 0:224], device)

    def half_y_sum():
        for i in (1, 2, 0):
            got(f"y2{i}")
        total = halved(y)
        for i in range(3):
            total = total + yr2[2, i, 0:224].astype(F32)
        for i in range(2):
            half_sum[i] = total[i * 112 : (i + 1) * 112]
        xs1[2, 0:112] = half_sum[1 - xl].astype(BF16)
        send("x2", xs1.at[2, 0:112], xr1.at[2, 0:112], xpt)

    def half_x():
        rows = pl.ds(pl.multiple_of((1 - xl) * 224 + 112, 16), 112)
        for n in range(4):
            xs4[1, n, 0:112] = acc[2, n, rows].astype(BF16)
        send("x4", xs4.at[1, :, 0:112], xr4.at[1, :, 0:112], xpt)

    def half_x_sum():
        got("x4")
        rows = pl.ds(pl.multiple_of(xl * 224 + 112, 16), 112)
        for n in range(4):
            accx[1, n, 0:112] = acc[2, n, rows] + xr4[1, n, 0:112].astype(F32)
        for i, (v, device) in enumerate(((y2, yfar), (yp, yup), (ym, ydn))):
            ys2[1, i, 224:336] = accx[1, v, 0:112].astype(BF16)
            send(f"y4{i}", ys2.at[1, i, 224:336], yr2.at[1, i, 224:336], device)

    def half_x_done():
        for i in (1, 2, 0):
            got(f"y4{i}")
        total = accx[1, y, 0:112]
        for i in range(3):
            total = total + yr2[1, i, 224:336].astype(F32)
        put_grad_one(2, total, 14, 27)

    grad_one((0,))
    send("df", own_delta, own_delta, zfar)
    add_sibling(0)
    ring_first(0, acc.at[0], 448)
    for way, _, _ in ways:
        got("e" + way)
    cells = pl.ds(pl.multiple_of(z * 128, 128), 128)
    flat = hid[cells, :].astype(F32).T.astype(BF16)
    for owner in range(16):
        gh[owner] = flat[owner * 32 : (owner + 1) * 32]
    for d in range(1, 16):
        send(f"g{d}", gh.at[around[d]], hh.at[z, s], {"space": around[d]})
    hh[z, s] = gh[s]
    got("dp")
    got("dm")
    for n in range(1, 4):
        for way, device, v in ways:
            block = quarter(lax.rem(v + n, 4))
            send(f"h{way}{n}", block, block, device)
    grad_one((1, 3))
    ring_second(0, acc.at[0], 448)
    add_sibling(1)
    x_first(1, 0)
    add_sibling(3)
    straight(3, acc.at[3], 448)
    got("df")
    grad_one((2,))
    for d in range(1, 16):
        got(f"g{d}")
    for way, device, _ in ways:
        send("v" + way, hh.at[z], hh.at[z], device)
    add_sibling(2)
    half_x()
    half_y()
    ring_third(0, acc.at[0], 448)
    x_last(0, 0)
    for n in range(1, 4):
        for way, _, _ in ways:
            got(f"h{way}{n}")

    fs[...] = jnp.zeros_like(fs)
    for later in range(2):
        for d in range(4):
            total = None
            for tap in range(27):
                do, di, dj = tap_shift(tap)
                if do != later or di * 2 + dj != d:
                    continue
                phase = tap_phase(tap)
                term = jnp.dot(
                    hid[phase * 64 : (phase + 1) * 64, :],
                    k2_v[tap * 512 : (tap + 1) * 512, :],
                    preferred_element_type=F32,
                )
                total = term if total is None else total + term
            fs[later, d, 1:9, 8:16, :] = total.reshape(8, 8, 256)
    for later in range(2):
        total = None
        for d in range(4):
            di, dj = d // 2, d % 2
            term = fs[later, d, 1 - di : 9 - di, 8 - dj : 16 - dj, :]
            total = term if total is None else total + term
        fp[later] = total.reshape(64, 256)
    send("f1", fp.at[1], fr, nxt)

    straight_sum(3, acc.at[3], 448)
    x_last(3, 1)
    x_second(1, 0)
    straight(1, accx.at[0], 224)
    half_y_sum()
    half_x_sum()
    got("f1")
    whole = fp[0] + jnp.where(s > 0, fr[...], 0.0)
    for half in range(2):
        fx[half] = whole[:, half * 128 : (half + 1) * 128]
    send("f2", fx.at[1 - h], fxr, hpt)

    for way in "pmf":
        got("v" + way)
    for phase in range(8):
        zz, e = phase // 2, phase % 2
        for m in range(8):
            two_slabs = [hh[zz, 2 * m + i, :, e * 64 : (e + 1) * 64] for i in range(2)]
            hp[phase * 32 : (phase + 1) * 32, m * 128 : (m + 1) * 128] = jnp.concatenate(two_slabs, 1)
    for do in range(2):
        for d in range(4):
            di, dj = d // 2, d % 2
            grads = jnp.dot(hp[...], up_s[d, do * 64 : do * 64 + 1024, :], preferred_element_type=F32)
            for tap in range(27):
                if tap_shift(tap) == (do, di, dj):
                    phase = tap_phase(tap)
                    g2_v[tap] = grads[phase * 32 : (phase + 1) * 32]
    stores = [pltpu.make_async_copy(g2_v, g2_o, lsem.at[4])]
    stores[0].start()

    x_done(0, 0)
    x_done(3, 1)
    straight_sum(1, accx.at[0], 224)
    put_grad_one(1, accx[0, y])
    got("x2")
    put_grad_one(2, half_sum[xl] + xr1[2, 0:112].astype(F32), 0, 14)
    half_x_done()
    stores.append(pltpu.make_async_copy(g1_v, g1_o, lsem.at[5]))
    stores[1].start()
    got("f2")
    feat_v[...] = fx[h] + fxr[...]
    stores.append(pltpu.make_async_copy(feat_v, feat_o, lsem.at[6]))
    stores[2].start()
    for message in msgs.values():
        message.wait_send()
    for copy in stores:
        copy.wait()


def place(feat, g1, g2, feat_o, g1_o, g2_o):
    feat_o[...] = feat[...]
    g1_o[...] = g1[...]
    g2_o[...] = g2[...]


def local(volume, kernel_one, kernel_two, upstream):
    any_spec = pl.BlockSpec(memory_space=pl.ANY)
    v = pltpu.VMEM
    shapes = (
        jax.ShapeDtypeStruct((64, 128), F32),
        jax.ShapeDtypeStruct((27, 8, 512), F32),
        jax.ShapeDtypeStruct((27, 32, 256), F32),
    )
    place_specs = (
        pl.BlockSpec((64, 128), lambda i: (0, 0)),
        pl.BlockSpec((9, 8, 512), lambda i: (i, 0, 0)),
        pl.BlockSpec((9, 32, 256), lambda i: (i, 0, 0)),
    )
    results = pl.pallas_call(
        body,
        out_shape=shapes,
        in_specs=[any_spec] * 4,
        out_specs=(any_spec,) * 3,
        scratch_shapes=[
            v((4, 32, 32, 128), BF16),
            v((32, 32, 128), BF16),
            v((3456, 512), BF16),
            v((27 * 512, 256), BF16),
            v((5, 33, 40, 128), F32),
            v((512, 3456), BF16),
            v((2, 4, 448, 512), BF16),
            v((2, 16, 64, 128), BF16),
            v((2, 64, 128), BF16),
            v((9, 16, 256), F32),
            v((4, 1088, 256), BF16),
            v((2, 4, 64, 256), BF16),
            v((4, 512, 128), F32),
            v((256, 128), F32),
            v((256, 128), F32),
            v((2, 512, 128), F32),
            v((4, 512, 128), F32),
            v((512, 128), BF16),
            v((2, 512, 128), BF16),
            v((2, 256, 128), BF16),
            v((2, 512, 128), BF16),
            v((512, 512), BF16),
            v((512, 512), BF16),
            v((4, 4, 448, 128), F32),
            v((4, 4, 448, 128), BF16),
            v((4, 4, 448, 128), BF16),
            v((2, 4, 224, 128), F32),
            v((2, 4, 224, 128), BF16),
            v((2, 4, 224, 128), BF16),
            v((3, 224, 128), BF16),
            v((3, 224, 128), BF16),
            v((2, 112, 128), F32),
            v((448, 128), BF16),
            v((2, 224, 128), BF16),
            v((4, 3, 448, 128), BF16),
            v((4, 3, 448, 128), BF16),
            v((16, 32, 128), BF16),
            v((4, 16, 32, 128), BF16),
            v((256, 1024), BF16),
            v((2, 4, 9, 16, 256), F32),
            v((2, 64, 256), F32),
            v((64, 256), F32),
            v((2, 64, 128), F32),
            v((64, 128), F32),
            v((64, 128), F32),
            v((27, 8, 512), F32),
            v((27, 32, 256), F32),
            pltpu.SemaphoreType.DMA((7,)),
            pltpu.SemaphoreType.DMA((NMSG,)),
            pltpu.SemaphoreType.DMA((NMSG,)),
        ],
        compiler_params=pltpu.CompilerParams(
            collective_id=0, has_side_effects=True, vmem_limit_bytes=60 * 1024 * 1024
        ),
        cost_estimate=pl.CostEstimate(flops=6_000_000_000, bytes_accessed=14_000_000, transcendentals=0),
        name="two_layers",
    )(
        volume,
        kernel_one.reshape(27 * 128, 512),
        kernel_two.reshape(27 * 512, 256),
        upstream.reshape(64, 128),
    )
    feat, g1, g2 = pl.pallas_call(
        place,
        out_shape=shapes,
        grid=(3,),
        in_specs=place_specs,
        out_specs=place_specs,
        name="place",
    )(*results)
    return feat.reshape(1, 8, 8, 128), g1, g2


def solution(mesh):
    return jax.shard_map(
        local,
        mesh=mesh,
        in_specs=(
            P("space", None, None, "chan"),
            P(None, "chan", "filt"),
            P(None, "filt", "chan"),
            P("space", None, None, ("chan", "filt")),
        ),
        out_specs=(
            P("space", None, None, ("chan", "filt")),
            P(None, ("chan", "space"), "filt"),
            P(None, ("filt", "space"), "chan"),
        ),
        check_vma=False,
    )
```

```python
import jax
import jax.numpy as jnp
from jax import lax
from jax.experimental import pallas as pl
from jax.experimental.pallas import tpu as pltpu
from jax.sharding import PartitionSpec as P

SLOPE = 0.3
F32, BF16 = jnp.float32, jnp.bfloat16
MESH = pl.DeviceIdType.MESH
NMSG = 96


def tap_parts(tap):
    return tap // 9, (tap // 3) % 3, tap % 3


def tap_phase(tap):
    a, b, c = tap_parts(tap)
    return ((a != 1) * 2 + (b != 1)) * 2 + (c != 1)


def tap_shift(tap):
    return tuple(int(v == 0) for v in tap_parts(tap))


def body(
    vol, k1, k2, up, feat_o, g1_o, g2_o,
    vol_v, halo_v, k1_v, k2_v, pf, patch, patch_t,
    up_all, up_next, up_f, up_s, seed_s,
    part, mr1, mrf, mr2, bpart, bs1, bs2, br1, br2,
    hid, dlt,
    acc, ksend, krecv, accx, xs4, xr4, xs1, xr1, half_sum, ys1, yr1, ys2, yr2,
    gh, hh, hp, fs, fp, fr, fx, fxr, feat_v, g1_v, g2_v,
    lsem, ssem, rsem,
):
    s, z, h = lax.axis_index("space"), lax.axis_index("chan"), lax.axis_index("filt")
    k, pair = lax.rem(s, 2), lax.div(s, 2)
    xl, y = lax.rem(pair, 2), lax.div(pair, 2)
    zp, zm, z2 = lax.rem(z + 1, 4), lax.rem(z + 3, 4), lax.rem(z + 2, 4)
    yp, ym, y2 = lax.rem(y + 1, 4), lax.rem(y + 3, 4), lax.rem(y + 2, 4)
    around = [lax.rem(s + d, 16) for d in range(16)]
    sib = {"space": s + 1 - 2 * k}
    xpt = {"space": y * 4 + (1 - xl) * 2 + k}
    hpt = {"filt": 1 - h}
    yup, ydn, yfar = ({"space": v * 4 + xl * 2 + k} for v in (yp, ym, y2))
    zup, zdn, zfar = {"chan": zp}, {"chan": zm}, {"chan": z2}
    nxt, prv = {"space": around[1]}, {"space": around[15]}
    nxt_h, prv_h = {"space": around[1], "filt": 1 - h}, {"space": around[15], "filt": 1 - h}

    msgs = {}

    def send(name, src, dst, device):
        i = len(msgs)
        msgs[name] = pltpu.make_async_remote_copy(
            src_ref=src, dst_ref=dst, send_sem=ssem.at[i], recv_sem=rsem.at[i], device_id=device, device_id_type=MESH
        )
        msgs[name].start()

    def got(name):
        msgs[name].wait_recv()

    def lanes(q):
        return pl.ds(pl.multiple_of(q * 128, 128), 128)

    loads = [
        pltpu.make_async_copy(vol, vol_v, lsem.at[0]),
        pltpu.make_async_copy(up, up_all.at[h, s], lsem.at[1]),
        pltpu.make_async_copy(k1, k1_v, lsem.at[2]),
        pltpu.make_async_copy(k2, k2_v, lsem.at[3]),
    ]
    for copy in loads[0:3]:
        copy.start()

    barrier = pltpu.get_barrier_semaphore()
    greeted = [{"space": v} for v in around[1:]] + [zup, zdn, zfar, hpt, nxt_h, prv_h]
    for device in greeted:
        pl.semaphore_signal(barrier, inc=1, device_id=device, device_id_type=MESH)
    pl.semaphore_wait(barrier, len(greeted))

    loads[1].wait()
    send("u0", up_all.at[h, s], up_all.at[h, s], hpt)
    send("u1", up_all.at[h, s], up_next.at[h], prv)
    send("u2", up_all.at[h, s], up_next.at[h], prv_h)
    loads[0].wait()
    send("halo", vol_v.at[3], halo_v, nxt)
    loads[3].start()

    zero_row = jnp.zeros((40, 128), F32)
    zero_col = jnp.zeros((33, 8, 128), F32)
    for p in range(5):
        pf[p, 0] = zero_row
        pf[p, :, 0:8, :] = zero_col

    def widen(r, carry):
        for p in range(4):
            pf[p + 1, r + 1, 8:40, :] = vol_v[p, r].astype(F32)
        return carry

    lax.fori_loop(0, 32, widen, 0)

    def build(o, depth_taps):
        def step(n, carry):
            pi, ii = lax.div(n, 4), lax.rem(n, 4)
            for pj in range(2):
                base = pl.multiple_of((o * 4 + pi * 2 + pj) * 64 + ii * 16, 16)
                for a in depth_taps:
                    for b in range(3):
                        row = 8 * ii + 2 * pi + b
                        for c in range(3):
                            tap = 9 * a + 3 * b + c
                            cols = pl.ds(7 + 2 * pj + c, 8, stride=4)
                            both = [pf[2 * o + a, row + 4 * e, cols, :] for e in range(2)]
                            patch[pl.ds(base, 16), tap * 128 : (tap + 1) * 128] = jnp.concatenate(both, 0).astype(BF16)
            return carry

        lax.fori_loop(0, 8, step, 0)

    build(1, (0, 1, 2))
    loads[2].wait()
    low, high = pl.ds(0, 256), pl.ds(256, 256)

    def conv_one(first, second, rows):
        weights = jnp.concatenate([k1_v[:, lanes(lax.rem(z + away, 4))] for away in (first, second)], 1)
        both = jnp.dot(patch[rows, :], weights, preferred_element_type=F32)
        part[first, rows, :] = both[:, 0:128]
        part[second, rows, :] = both[:, 128:256]

    conv_one(2, 1, high)
    send("m1m", part.at[2, high], mr1, zdn)
    send("m2pb", part.at[1, high], mr2.at[0, high], zup)
    conv_one(3, 0, high)
    build(0, (1, 2))

    up_f[...] = jnp.zeros_like(up_f)

    def moved(blocks, store):
        for half in range(2):
            up_f[0:8, 0:8, half * 128 : (half + 1) * 128] = blocks[half].astype(F32).reshape(8, 8, 128)
        for di in range(2):
            for dj in range(2):
                store(di * 2 + dj, up_f[di : di + 8, dj : dj + 8, :].reshape(64, 256).astype(BF16))

    got("u0")
    got("u1")
    got("u2")
    def store_seed(later):
        def store(d, value):
            seed_s[later, d] = value

        return store

    moved([up_all[half, s] for half in range(2)], store_seed(0))
    moved([jnp.where(s < 15, up_next[half].astype(F32), 0.0) for half in range(2)], store_seed(1))

    loads[3].wait()
    for phase in range(8):
        total = None
        for tap in range(27):
            if tap_phase(tap) != phase:
                continue
            do, di, dj = tap_shift(tap)
            term = lax.dot_general(
                seed_s[do, di * 2 + dj],
                k2_v[tap * 512 : (tap + 1) * 512, :],
                (((1,), (1,)), ((), ())),
                preferred_element_type=F32,
            )
            total = term if total is None else total + term
        for q in range(4):
            bpart[q, phase * 64 : (phase + 1) * 64, :] = total[:, q * 128 : (q + 1) * 128]
    bs1[...] = bpart[z2].astype(BF16)
    send("b1p", bs1.at[low], br1.at[0], zup)
    send("b1m", bs1.at[high], br1.at[1], zdn)
    bs2[0, 256:512] = bpart[zp, 256:512].astype(BF16)
    send("b2pb", bs2.at[0, high], br2.at[0, high], zup)
    bs2[1, 0:256] = bpart[zm, 0:256].astype(BF16)
    send("b2ma", bs2.at[1, low], br2.at[1, low], zdn)

    got("halo")

    def widen_halo(r, carry):
        pf[0, r + 1, 8:40, :] = jnp.where(s > 0, halo_v[r].astype(F32), 0.0)
        return carry

    lax.fori_loop(0, 32, widen_halo, 0)
    build(0, (0,))
    conv_one(2, 3, low)
    send("m1p", part.at[2, low], mrf, zup)
    send("m2ma", part.at[3, low], mr2.at[1, low], zdn)
    own_pair = up_all.at[:, s]
    for d in range(1, 16):
        send(f"a{d}", own_pair, own_pair, {"space": around[d]})
    got("m1m")
    part[3, 256:512] += mr1[...]
    send("m2mb", part.at[3, high], mr2.at[1, high], zdn)
    conv_one(1, 0, low)
    got("b1p")
    bs2[0, 0:256] = (bpart[zp, 0:256] + br1[0].astype(F32)).astype(BF16)
    send("b2pa", bs2.at[0, low], br2.at[0, low], zup)
    got("b1m")
    bs2[1, 256:512] = (bpart[zm, 256:512] + br1[1].astype(F32)).astype(BF16)
    send("b2mb", bs2.at[1, high], br2.at[1, high], zdn)
    got("m1p")
    part[1, 0:256] += mrf[...]
    send("m2pa", part.at[1, low], mr2.at[0, low], zup)

    def put_turned(flat_rows, rows_at):
        for owner in range(16):
            yd, xd, kd = owner // 4, (owner // 2) % 2, owner % 2
            patch_t[kd, yd, pl.ds(pl.multiple_of(rows_at + xd * 224, 16), 16), :] = flat_rows(owner).astype(BF16)

    def turn(n, carry):
        flat = patch[:, pl.ds(pl.multiple_of(n * 256, 256), 256)].astype(F32).T

        def two_taps(owner):
            return jnp.concatenate([flat[e * 128 + owner * 8 : e * 128 + owner * 8 + 8] for e in range(2)], 0)

        put_turned(two_taps, n * 16)
        return carry

    lax.fori_loop(0, 13, turn, 0)
    flat = patch[:, 26 * 128 : 27 * 128].astype(F32).T
    put_turned(lambda owner: jnp.concatenate([flat[owner * 8 : owner * 8 + 8], jnp.zeros((8, 512), F32)], 0), 208)

    for name in ("m2pb", "m2ma", "m2mb", "m2pa"):
        got(name)
    mixed = part[0] + mr2[0] + mr2[1]
    part[0] = mixed
    hid[:, lanes(z)] = jnp.where(mixed > 0, mixed, SLOPE * mixed).astype(BF16)
    ways = (("p", zup, zp), ("m", zdn, zm), ("f", zfar, z2))

    def quarter(v):
        return hid.at[pl.ds(pl.multiple_of(v * 128, 128), 128), lanes(z)]

    for way, device, v in ways:
        send("e" + way, quarter(v), quarter(v), device)
    for name in ("b2pb", "b2ma", "b2pa", "b2mb"):
        got(name)
    back = bpart[z] + br2[0].astype(F32) + br2[1].astype(F32)
    dlt[:, lanes(z)] = (back * jnp.where(part[0] > 0, 1.0, SLOPE)).astype(BF16)
    own_delta = dlt.at[:, lanes(z)]
    send("dp", own_delta, own_delta, zup)
    send("dm", own_delta, own_delta, zdn)

    def grad_one(slots):
        deltas = jnp.concatenate([dlt[:, lanes(lax.rem(z + slot, 4))] for slot in slots], 1)
        for yd in range(4):
            term = jnp.dot(patch_t[1 - k, yd], deltas, preferred_element_type=F32)
            for i, slot in enumerate(slots):
                ksend[slot, yd] = term[:, i * 128 : (i + 1) * 128].astype(BF16)
        for slot in slots:
            send(f"k{slot}", ksend.at[slot], krecv.at[slot], sib)
        for yd in range(4):
            term = jnp.dot(patch_t[k, yd], deltas, preferred_element_type=F32)
            for i, slot in enumerate(slots):
                acc[slot, yd] = term[:, i * 128 : (i + 1) * 128]

    def add_sibling(slot):
        got(f"k{slot}")

        def step(n, carry):
            acc[slot, n] += krecv[slot, n].astype(F32)
            return carry

        lax.fori_loop(0, 4, step, 0)

    def ring_first(slot, ref, rows):
        half = rows // 2
        ys1[0:rows] = ref[y2].astype(BF16)
        send(f"p{slot}", ys1.at[0:half], yr1.at[0, 0:half], yup)
        send(f"q{slot}", ys1.at[half:rows], yr1.at[1, 0:half], ydn)

    def ring_second(slot, ref, rows):
        half = rows // 2
        got(f"p{slot}")
        ys2[slot, 0, 0:half] = (ref[yp, 0:half] + yr1[0, 0:half].astype(F32)).astype(BF16)
        ys2[slot, 0, half:rows] = ref[yp, half:rows].astype(BF16)
        send(f"r{slot}", ys2.at[slot, 0, 0:rows], yr2.at[slot, 0, 0:rows], yup)
        got(f"q{slot}")
        ys2[slot, 1, 0:half] = ref[ym, 0:half].astype(BF16)
        ys2[slot, 1, half:rows] = (ref[ym, half:rows] + yr1[1, 0:half].astype(F32)).astype(BF16)
        send(f"t{slot}", ys2.at[slot, 1, 0:rows], yr2.at[slot, 1, 0:rows], ydn)

    def ring_third(slot, ref, rows):
        got(f"r{slot}")
        got(f"t{slot}")
        ref[y, 0:rows] = ref[y, 0:rows] + yr2[slot, 0, 0:rows].astype(F32) + yr2[slot, 1, 0:rows].astype(F32)

    def straight(slot, ref, rows):
        for i, (v, device) in enumerate(((y2, yfar), (yp, yup), (ym, ydn))):
            ys2[slot, i, 0:rows] = ref[v].astype(BF16)
            send(f"y{slot}{i}", ys2.at[slot, i, 0:rows], yr2.at[slot, i, 0:rows], device)

    def straight_sum(slot, ref, rows):
        for i in (1, 2, 0):
            got(f"y{slot}{i}")
        total = ref[y, 0:rows]
        for i in range(3):
            total = total + yr2[slot, i, 0:rows].astype(F32)
        ref[y, 0:rows] = total

    mine = pl.ds(pl.multiple_of(xl * 224, 32), 224)
    other = pl.ds(pl.multiple_of((1 - xl) * 224, 32), 224)

    def put_grad_one(slot, value, first=0, last=27):
        q = lax.rem(z + slot, 4)
        g1_v[first:last, :, lanes(q)] = value[0 : (last - first) * 8].reshape(last - first, 8, 128)

    def x_first(slot, lane):
        for n in range(4):
            xs4[lane, n] = acc[slot, n, other].astype(BF16)
        send(f"x{slot}", xs4.at[lane], xr4.at[lane], xpt)

    def x_second(slot, lane):
        got(f"x{slot}")
        for n in range(4):
            accx[lane, n] = acc[slot, n, mine] + xr4[lane, n].astype(F32)

    def x_last(slot, lane):
        xs1[lane] = acc[slot, y, other].astype(BF16)
        send(f"x{slot}", xs1.at[lane], xr1.at[lane], xpt)

    def x_done(slot, lane):
        got(f"x{slot}")
        put_grad_one(slot, acc[slot, y, mine] + xr1[lane].astype(F32))

    def halved(v):
        return jnp.concatenate([acc[2, v, 0:112], acc[2, v, 224:336]], 0)

    def half_y():
        for i, (v, device) in enumerate(((y2, yfar), (yp, yup), (ym, ydn))):
            ys2[2, i, 0:224] = halved(v).astype(BF16)
            send(f"y2{i}", ys2.at[2, i, 0:224], yr2.at[2, i, 0:224], device)

    def half_y_sum():
        for i in (1, 2, 0):
            got(f"y2{i}")
        total = halved(y)
        for i in range(3):
            total = total + yr2[2, i, 0:224].astype(F32)
        for i in range(2):
            half_sum[i] = total[i * 112 : (i + 1) * 112]
        xs1[2, 0:112] = half_sum[1 - xl].astype(BF16)
        send("x2", xs1.at[2, 0:112], xr1.at[2, 0:112], xpt)

    def half_x():
        rows = pl.ds(pl.multiple_of((1 - xl) * 224 + 112, 16), 112)
        for n in range(4):
            xs4[1, n, 0:112] = acc[2, n, rows].astype(BF16)
        send("x4", xs4.at[1, :, 0:112], xr4.at[1, :, 0:112], xpt)

    def half_x_sum():
        got("x4")
        rows = pl.ds(pl.multiple_of(xl * 224 + 112, 16), 112)
        for n in range(4):
            accx[1, n, 0:112] = acc[2, n, rows] + xr4[1, n, 0:112].astype(F32)
        for i, (v, device) in enumerate(((y2, yfar), (yp, yup), (ym, ydn))):
            ys2[1, i, 224:336] = accx[1, v, 0:112].astype(BF16)
            send(f"y4{i}", ys2.at[1, i, 224:336], yr2.at[1, i, 224:336], device)

    def half_x_done():
        for i in (1, 2, 0):
            got(f"y4{i}")
        total = accx[1, y, 0:112]
        for i in range(3):
            total = total + yr2[1, i, 224:336].astype(F32)
        put_grad_one(2, total, 14, 27)

    grad_one((0,))
    send("df", own_delta, own_delta, zfar)
    add_sibling(0)
    ring_first(0, acc.at[0], 448)
    for way, _, _ in ways:
        got("e" + way)
    cells = pl.ds(pl.multiple_of(z * 128, 128), 128)
    flat = hid[cells, :].astype(F32).T.astype(BF16)
    for owner in range(16):
        gh[owner] = flat[owner * 32 : (owner + 1) * 32]
    for d in range(1, 16):
        send(f"g{d}", gh.at[around[d]], hh.at[z, s], {"space": around[d]})
    hh[z, s] = gh[s]
    got("dp")
    got("dm")
    for n in range(1, 4):
        for way, device, v in ways:
            block = quarter(lax.rem(v + n, 4))
            send(f"h{way}{n}", block, block, device)
    grad_one((1, 3))
    ring_second(0, acc.at[0], 448)
    add_sibling(1)
    x_first(1, 0)
    add_sibling(3)
    straight(3, acc.at[3], 448)
    got("df")
    grad_one((2,))
    for d in range(1, 16):
        got(f"g{d}")
    for way, device, _ in ways:
        send("v" + way, hh.at[z], hh.at[z], device)
    add_sibling(2)
    half_x()
    half_y()
    ring_third(0, acc.at[0], 448)
    x_last(0, 0)
    for d in range(4):
        up_s[d, 1024:1088, :] = jnp.zeros((64, 256), BF16)
    for d in range(1, 16):
        got(f"a{d}")

    def shifted(slab, carry):
        def store(d, value):
            up_s[d, pl.ds(pl.multiple_of(slab * 64, 64), 64), :] = value

        moved([up_all[half, slab] for half in range(2)], store)
        return carry

    lax.fori_loop(0, 16, shifted, 0)

    for n in range(1, 4):
        for way, _, _ in ways:
            got(f"h{way}{n}")

    fs[...] = jnp.zeros_like(fs)
    for later in range(2):
        for d in range(4):
            total = None
            for tap in range(27):
                do, di, dj = tap_shift(tap)
                if do != later or di * 2 + dj != d:
                    continue
                phase = tap_phase(tap)
                term = jnp.dot(
                    hid[phase * 64 : (phase + 1) * 64, :],
                    k2_v[tap * 512 : (tap + 1) * 512, :],
                    preferred_element_type=F32,
                )
                total = term if total is None else total + term
            fs[later, d, 1:9, 8:16, :] = total.reshape(8, 8, 256)
    for later in range(2):
        total = None
        for d in range(4):
            di, dj = d // 2, d % 2
            term = fs[later, d, 1 - di : 9 - di, 8 - dj : 16 - dj, :]
            total = term if total is None else total + term
        fp[later] = total.reshape(64, 256)
    send("f1", fp.at[1], fr, nxt)

    straight_sum(3, acc.at[3], 448)
    x_last(3, 1)
    x_second(1, 0)
    straight(1, accx.at[0], 224)
    half_y_sum()
    half_x_sum()
    got("f1")
    whole = fp[0] + jnp.where(s > 0, fr[...], 0.0)
    for half in range(2):
        fx[half] = whole[:, half * 128 : (half + 1) * 128]
    send("f2", fx.at[1 - h], fxr, hpt)

    for way in "pmf":
        got("v" + way)
    for phase in range(8):
        zz, e = phase // 2, phase % 2
        for m in range(8):
            two_slabs = [hh[zz, 2 * m + i, :, e * 64 : (e + 1) * 64] for i in range(2)]
            hp[phase * 32 : (phase + 1) * 32, m * 128 : (m + 1) * 128] = jnp.concatenate(two_slabs, 1)
    for do in range(2):
        for d in range(4):
            di, dj = d // 2, d % 2
            grads = jnp.dot(hp[...], up_s[d, do * 64 : do * 64 + 1024, :], preferred_element_type=F32)
            for tap in range(27):
                if tap_shift(tap) == (do, di, dj):
                    phase = tap_phase(tap)
                    g2_v[tap] = grads[phase * 32 : (phase + 1) * 32]
    stores = [pltpu.make_async_copy(g2_v, g2_o, lsem.at[4])]
    stores[0].start()

    x_done(0, 0)
    x_done(3, 1)
    straight_sum(1, accx.at[0], 224)
    put_grad_one(1, accx[0, y])
    got("x2")
    put_grad_one(2, half_sum[xl] + xr1[2, 0:112].astype(F32), 0, 14)
    half_x_done()
    stores.append(pltpu.make_async_copy(g1_v, g1_o, lsem.at[5]))
    stores[1].start()
    got("f2")
    feat_v[...] = fx[h] + fxr[...]
    stores.append(pltpu.make_async_copy(feat_v, feat_o, lsem.at[6]))
    stores[2].start()
    for message in msgs.values():
        message.wait_send()
    for copy in stores:
        copy.wait()


def place(*refs):
    sources, targets, sems = refs[0:3], refs[3:6], refs[6]
    copies = [pltpu.make_async_copy(a, b, sems.at[i]) for i, (a, b) in enumerate(zip(sources, targets))]
    for copy in copies:
        copy.start()
    for copy in copies:
        copy.wait()


def local(volume, kernel_one, kernel_two, upstream):
    any_spec = pl.BlockSpec(memory_space=pl.ANY)
    v = pltpu.VMEM
    shapes = (
        jax.ShapeDtypeStruct((64, 128), F32),
        jax.ShapeDtypeStruct((27, 8, 512), F32),
        jax.ShapeDtypeStruct((27, 32, 256), F32),
    )
    results = pl.pallas_call(
        body,
        out_shape=shapes,
        in_specs=[any_spec] * 4,
        out_specs=(any_spec,) * 3,
        scratch_shapes=[
            v((4, 32, 32, 128), BF16),
            v((32, 32, 128), BF16),
            v((3456, 512), BF16),
            v((27 * 512, 256), BF16),
            v((5, 33, 40, 128), F32),
            v((512, 3456), BF16),
            v((2, 4, 448, 512), BF16),
            v((2, 16, 64, 128), BF16),
            v((2, 64, 128), BF16),
            v((9, 16, 256), F32),
            v((4, 1088, 256), BF16),
            v((2, 4, 64, 256), BF16),
            v((4, 512, 128), F32),
            v((256, 128), F32),
            v((256, 128), F32),
            v((2, 512, 128), F32),
            v((4, 512, 128), F32),
            v((512, 128), BF16),
            v((2, 512, 128), BF16),
            v((2, 256, 128), BF16),
            v((2, 512, 128), BF16),
            v((512, 512), BF16),
            v((512, 512), BF16),
            v((4, 4, 448, 128), F32),
            v((4, 4, 448, 128), BF16),
            v((4, 4, 448, 128), BF16),
            v((2, 4, 224, 128), F32),
            v((2, 4, 224, 128), BF16),
            v((2, 4, 224, 128), BF16),
            v((3, 224, 128), BF16),
            v((3, 224, 128), BF16),
            v((2, 112, 128), F32),
            v((448, 128), BF16),
            v((2, 224, 128), BF16),
            v((4, 3, 448, 128), BF16),
            v((4, 3, 448, 128), BF16),
            v((16, 32, 128), BF16),
            v((4, 16, 32, 128), BF16),
            v((256, 1024), BF16),
            v((2, 4, 9, 16, 256), F32),
            v((2, 64, 256), F32),
            v((64, 256), F32),
            v((2, 64, 128), F32),
            v((64, 128), F32),
            v((64, 128), F32),
            v((27, 8, 512), F32),
            v((27, 32, 256), F32),
            pltpu.SemaphoreType.DMA((7,)),
            pltpu.SemaphoreType.DMA((NMSG,)),
            pltpu.SemaphoreType.DMA((NMSG,)),
        ],
        compiler_params=pltpu.CompilerParams(
            collective_id=0, has_side_effects=True, vmem_limit_bytes=60 * 1024 * 1024
        ),
        cost_estimate=pl.CostEstimate(flops=6_000_000_000, bytes_accessed=14_000_000, transcendentals=0),
        name="two_layers",
    )(
        volume,
        kernel_one.reshape(27 * 128, 512),
        kernel_two.reshape(27 * 512, 256),
        upstream.reshape(64, 128),
    )
    feat, g1, g2 = pl.pallas_call(
        place,
        out_shape=shapes,
        in_specs=[pl.BlockSpec(memory_space=pltpu.VMEM)] * 3,
        out_specs=(any_spec,) * 3,
        scratch_shapes=[pltpu.SemaphoreType.DMA((3,))],
        name="place",
    )(*results)
    return feat.reshape(1, 8, 8, 128), g1, g2


def solution(mesh):
    return jax.shard_map(
        local,
        mesh=mesh,
        in_specs=(
            P("space", None, None, "chan"),
            P(None, "chan", "filt"),
            P(None, "filt", "chan"),
            P("space", None, None, ("chan", "filt")),
        ),
        out_specs=(
            P("space", None, None, ("chan", "filt")),
            P(None, ("chan", "space"), "filt"),
            P(None, ("filt", "space"), "chan"),
        ),
        check_vma=False,
    )
```
